512 devices in a mesh: dp: 8 (over y, core), expert: 64 (over x, z).
Axes of the slice: x: 4, y: 4, z: 16, core: 2. Of those that a mesh axis runs over, the one named last changes fastest.
Arguments:
- tokens: bfloat16 [64, 64, 3584], P('expert', 'dp'), may hold values from -6 to 6
- grad_out: bfloat16 [64, 64, 3584], P('expert', 'dp'), may hold values from -6 to 6
- routes: int32 [64, 64, 8], P('expert', 'dp'), may hold values from 0 to 255, all different within a row; in each aligned block of 64 rows (0 to 63, 64 to 127, ..., all dimensions but the last counted through in order) at most 4 rows name the same one
- gate_scores: bfloat16 [64, 64, 8], P('expert', 'dp'), may hold values from 0.099609375 to 0.59765625
- w_gate: bfloat16 [64, 3584, 1024], P('expert', None, 'dp'), may hold values from -0.09375 to 0.09375
- w_up: bfloat16 [64, 3584, 1024], P('expert', None, 'dp'), may hold values from -0.09375 to 0.09375
- w_down: bfloat16 [64, 1024, 3584], P('expert', 'dp'), may hold values from -0.1875 to 0.1875
Outputs:
- grad_tokens: bfloat16 [64, 64, 3584], P('expert', 'dp')
- grad_gate: bfloat16 [64, 3584, 1024], P('expert', None, 'dp')
- grad_up: bfloat16 [64, 3584, 1024], P('expert', None, 'dp')
The draws below stay inside these ranges and needn't reach their ends.
Inputs may be any that keep to these rules, and one draw needn't show every extreme that they name: `routes`: each token names 8 different experts. In each token group of 64 tokens no expert is named by more than 4 tokens, a bound that some block reaches.
All inputs are finite; a program needn't handle non-finite values.
Results may differ from the reference program's by a relative error of at most 0.0058.
Values may be sent and summed in bfloat16 or wider, within the bound.
A program may use at most 64 MiB of HBM per device.

```python
import math
import jax
import jax.numpy as jnp
import numpy as np
from jax import lax

D = 3584
FF = 1024
ROUTED = 256
TOP = 8
EXPERTS = 64
COLUMNS = 64
TOK_COL = 64
MOST = 4


def steps_of(rng, extent, split, least, high):
    gain = 1.0
    for axis_at, blocks in split:
        steps = jax.random.uniform(jax.random.fold_in(jax.random.fold_in(rng, 6), axis_at), (blocks,), jnp.float32, least / len(split), high / len(split))
        gain = gain * jnp.repeat(jnp.exp(steps), extent[axis_at] // blocks).reshape((-1,) + (1,) * (len(extent) - 1 - axis_at))
    return gain


def deal_out(stream_key, own, number, rows, amount, top, limit, skew):
    order = jax.random.permutation(stream_key, amount)
    packed, common = portions_of(amount, rows * top, limit, skew, True), portions_of(amount, rows * top, limit, skew, False)
    places = jnp.arange(amount)

    def named(sizes, turn):
        used = int((sizes > 0).sum())
        fixed = max(1, used // 4)
        passed = fixed + (places - fixed + turn * (used - fixed)) % max(1, amount - fixed)
        return jnp.zeros((amount,), jnp.int32).at[order[jnp.where(places < fixed, places, passed)]].set(jnp.asarray(sizes, jnp.int32))

    sizes = jnp.where(number % 4 == 0, named(packed, number // 4), named(common, number - number // 4 - 1))
    mixed = jax.random.permutation(jax.random.fold_in(own, 3), amount)
    giver, sink = mixed[0:amount // 2 * 2:2], mixed[1:amount // 2 * 2:2]
    slack = jnp.minimum(sizes[giver] - 1, limit - sizes[sink]) // 2
    slack = jnp.where((giver == order[0]) | (sink == order[0]) | (sizes[sink] == 0), 0, jnp.maximum(slack, 0))
    passed = jax.random.randint(jax.random.fold_in(own, 4), (amount // 2,), 0, 1 << 20) % (slack + 1)
    sizes = sizes.at[giver].add(-passed).at[sink].add(passed)
    items = jnp.searchsorted(jnp.cumsum(sizes), jnp.arange(rows * top), side="right").astype(jnp.int32)
    listing = items.reshape(top, rows).T
    listing = listing[jax.random.permutation(jax.random.fold_in(own, 1), rows)]
    turn = jax.random.randint(jax.random.fold_in(own, 2), (rows, 1), 0, top)
    return jnp.take_along_axis(listing, (jnp.arange(top)[None, :] + turn) % top, axis=1)


def portions_of(number_of, total, bound, lean, full):
    weights = [(1 << 20) // math.isqrt(rank ** lean) + 1 for rank in range(1, number_of + 1)]
    largest = bound if full else min(bound, max(-(-total // number_of), total * weights[0] // sum(weights)))
    least = 1 if total - largest >= number_of - 1 else 0
    given, surplus = [largest] + [least] * (number_of - 1), total - largest - least * (number_of - 1)
    while surplus > 0:
        movable = [i for i in range(1, number_of) if given[i] < largest] or [i for i in range(1, number_of) if given[i] < bound]
        pool, budget = sum([weights[i] for i in movable]), surplus
        for i in movable:
            extra = min(bound - given[i], max(1, budget * weights[i] // pool), surplus)
            given[i] = given[i] + extra
            surplus = surplus - extra
    return np.array(given)


def noise(rng, dims, width, limit, shards=(), held_as=jnp.bfloat16):
    entries = jax.random.normal(rng, dims, jnp.float32) * width
    if len(shards) > 0:
        entries = steps_of(rng, dims, shards, -0.22, 0.18) * entries
    return jnp.clip(entries, min=-limit, max=limit).astype(held_as)


def setup_inputs(seed: int = 0) -> dict:
    streams_of = jax.random.split(jax.random.key(seed), 8)
    tokens = noise(streams_of[0], (COLUMNS, TOK_COL, D), 1.0, 6.0, ((0, 64), (1, 8)))
    grad_out = noise(streams_of[1], (COLUMNS, TOK_COL, D), 1.0, 6.0, ((0, 64), (1, 8)))
    routes_keys = jax.random.split(jax.random.fold_in(streams_of[2], 1), COLUMNS * TOK_COL // TOK_COL)
    routes_turns = jax.random.permutation(jax.random.fold_in(streams_of[2], 3), COLUMNS * TOK_COL // TOK_COL)
    routes = jax.vmap(lambda own, number: deal_out(jax.random.fold_in(streams_of[2], 2), own, number, TOK_COL, ROUTED, TOP, MOST, 2))(routes_keys, routes_turns).reshape((COLUMNS, TOK_COL, TOP))
    gate_scores = jnp.clip(0.099609375 + 0.49804688 * jax.random.uniform(streams_of[3], (COLUMNS, TOK_COL, TOP), jnp.float32) ** steps_of(streams_of[3], (COLUMNS, TOK_COL, TOP), ((0, 64), (1, 8)), -0.2, 0.2), 0.099609375, 0.59765625).astype(jnp.bfloat16)
    w_gate = noise(streams_of[4], (EXPERTS, D, FF), D ** -0.5, 0.09375, ((0, 64), (2, 8)))
    w_up = noise(streams_of[5], (EXPERTS, D, FF), D ** -0.5, 0.09375, ((0, 64), (2, 8)))
    w_down = noise(streams_of[6], (EXPERTS, FF, D), FF ** -0.5, 0.1875, ((0, 64), (1, 8)))
    return dict(tokens=tokens, grad_out=grad_out, routes=routes, gate_scores=gate_scores, w_gate=w_gate, w_up=w_up, w_down=w_down)


def reference(tokens, grad_out, routes, gate_scores, w_gate, w_up, w_down):
    flat_x = tokens.reshape(-1, D)
    flat_dy = grad_out.reshape(-1, D)
    flat_routes = routes.reshape(-1).astype(jnp.int32)
    flat_scores = gate_scores.reshape(-1).astype(jnp.float32)
    count = COLUMNS * MOST

    def per_expert(total, inputs):
        expert, wgate, wup, wdown = inputs
        hits = flat_routes == expert
        slot = jnp.nonzero(hits, size=count, fill_value=0)[0].astype(jnp.int32)
        valid = jnp.arange(count, dtype=jnp.int32) < jnp.sum(hits.astype(jnp.int32))
        token = (slot // TOP).astype(jnp.int32)
        rows = flat_x[token]
        weight = jnp.where(valid, flat_scores[slot], jnp.zeros((), jnp.float32))
        scaled = (weight[:, None] * flat_dy[token].astype(jnp.float32)).astype(jnp.bfloat16)
        gate = jnp.dot(rows, wgate, preferred_element_type=jnp.float32)
        up = jnp.dot(rows, wup, preferred_element_type=jnp.float32)
        dhidden = jnp.dot(scaled, wdown.T, preferred_element_type=jnp.float32)
        sig = jax.nn.sigmoid(gate)
        dgate = (dhidden * up * sig * (1.0 + gate * (1.0 - sig))).astype(jnp.bfloat16)
        dup = (dhidden * gate * sig).astype(jnp.bfloat16)
        grad_g = jnp.dot(rows.T, dgate, preferred_element_type=jnp.float32).astype(jnp.bfloat16)
        grad_u = jnp.dot(rows.T, dup, preferred_element_type=jnp.float32).astype(jnp.bfloat16)
        moved = jnp.dot(dgate, wgate.T, preferred_element_type=jnp.float32)
        moved = moved + jnp.dot(dup, wup.T, preferred_element_type=jnp.float32)
        moved = jnp.where(valid[:, None], moved, jnp.zeros((), jnp.float32))
        return total.at[token].add(moved), (grad_g, grad_u)

    start = jnp.zeros((COLUMNS * TOK_COL, D), jnp.float32)
    experts = jnp.arange(EXPERTS, dtype=jnp.int32)
    total, grads = lax.scan(per_expert, start, (experts, w_gate, w_up, w_down))
    grad_tokens = total.reshape(COLUMNS, TOK_COL, D).astype(jnp.bfloat16)
    return grad_tokens, grads[0], grads[1]
```

```python
import functools

import jax
import jax.numpy as jnp
from jax import lax
from jax.experimental import pallas as pl
from jax.experimental.pallas import tpu as pltpu
from jax.sharding import PartitionSpec as P

ROUTED = 256
CORES = 2
QUARTERS = 4
MESH = pl.DeviceIdType.MESH
F32, BF16 = jnp.float32, jnp.bfloat16
NT = (((1,), (1,)), ((), ()))
TN = (((0,), (0,)), ((), ()))


def shape_of(mesh_experts, columns_z, width, tok_col, top, hidden):
    z_size = columns_z
    x_size = mesh_experts // z_size
    most = max(2, 2 * tok_col * top // ROUTED)
    quarter = width // QUARTERS
    tiles = quarter // 128
    wide = (tiles + 1) // 2 * 128
    parts = min(4, z_size)
    return dict(
        xs=x_size, zs=z_size, most=most, qw=quarter, wide=wide, parts=parts,
        slots=mesh_experts // parts, experts=mesh_experts, toks=tok_col, top=top, hid=hidden,
    )


def kernel(
    c, tok_ref, dy_ref, routes_ref, scores_ref, wg_hbm, wu_hbm, wd_hbm,
    out_t, out_g, out_u,
    wcat, wd, sa, ra, si, ri, sb, rb, dd, keep, sr1, rr1, sr2, rr2, sr3, rr3, sf, rf, sel_ref,
    w_sem, sa_sem, ra_sem, si_sem, ri_sem, sb_sem, rb_sem,
    sy_sem, ry_sem, sc_sem, rc_sem, s1_sem, r1_sem, s2_sem, r2_sem, s3_sem, r3_sem,
    sf_sem, rf_sem,
):
    xs, zs, most, qw, wide, parts = c["xs"], c["zs"], c["most"], c["qw"], c["wide"], c["parts"]
    slots, experts, toks, hid = c["slots"], c["experts"], c["toks"], c["hid"]
    narrow = qw - wide
    rows = slots * most
    groups = CORES * QUARTERS
    per = toks // groups
    d = lax.axis_index("dp")
    e = lax.axis_index("expert")
    y, core = d // CORES, d % CORES
    x, z = e // zs, e % zs
    other = y * CORES + (1 - core)
    up_y, down_y = (y + 1) % QUARTERS, (y + QUARTERS - 1) % QUARTERS
    far_y = (y + 2) % QUARTERS
    up, down = up_y * CORES + core, down_y * CORES + core

    def remote(src, dst, send, recv, **where):
        return pltpu.make_async_remote_copy(
            src_ref=src, dst_ref=dst, send_sem=send, recv_sem=recv,
            device_id=where, device_id_type=MESH,
        )

    def landed(ref, sem):
        pltpu.make_async_copy(ref, ref, sem).wait()

    loads = [
        pltpu.make_async_copy(wg_hbm.at[0], wcat.at[:, 0:hid], w_sem.at[0]),
        pltpu.make_async_copy(wu_hbm.at[0], wcat.at[:, hid : 2 * hid], w_sem.at[1]),
        pltpu.make_async_copy(wd_hbm.at[0], wd, w_sem.at[2]),
    ]
    for load in loads:
        load.start()

    barrier = pltpu.get_barrier_semaphore()
    for j in range(1, groups):
        pl.semaphore_signal(
            barrier, inc=1, device_id={"dp": (d + j) % groups}, device_id_type=MESH
        )

    def greet(j, carry):
        pl.semaphore_signal(
            barrier, inc=1, device_id={"expert": (e + j) % experts}, device_id_type=MESH
        )
        return carry

    lax.fori_loop(1, experts, greet, 0)

    si[...] = jnp.zeros(si.shape, F32)
    si[0, :, 0 : c["top"]] = routes_ref[0].astype(F32)
    si[1, :, 0 : c["top"]] = scores_ref[0].astype(F32)
    for p in range(groups):
        source = tok_ref if p % CORES == 0 else dy_ref
        at = p // CORES * qw
        sa[p] = source[0, :, at : at + qw]
    ri[d] = si[...]
    ra[d] = sa[d]
    pl.semaphore_wait(barrier, groups - 1 + experts - 1)

    sent_i, sent_a = [], []
    for j in range(1, groups):
        p = (d + j) % groups
        sent_i.append(remote(si, ri.at[d], si_sem.at[j - 1], ri_sem.at[j - 1], dp=p))
        sent_i[-1].start()
    for j in range(1, groups):
        p = (d + j) % groups
        sent_a.append(remote(sa.at[p], ra.at[d], sa_sem.at[j - 1], ra_sem.at[j - 1], dp=p))
        sent_a[-1].start()
    for j in range(1, groups):
        landed(ri.at[(d + groups - j) % groups], ri_sem.at[j - 1])

    route = ri[:, 0].reshape(toks, 128)
    score = ri[:, 1].reshape(toks, 128)
    shape = (toks, experts * most)
    row = lax.broadcasted_iota(jnp.int32, shape, 1)
    place_of = row % most
    slot_of = row // most
    dx_of = slot_of % xs
    k_of = slot_of // xs
    dz_of = (k_of + 1) // 2 * (2 * (k_of % 2) - 1)
    target = ((x + dx_of) % xs * zs + (z + dz_of + zs) % zs).astype(F32)
    hit = jnp.zeros(shape, F32)
    weight = jnp.zeros(shape, F32)
    for k in range(c["top"]):
        same = route[:, k : k + 1] == target
        hit = jnp.where(same, 1.0, hit)
        weight = jnp.where(same, score[:, k : k + 1], weight)
    before = (
        lax.broadcasted_iota(jnp.int32, (toks, toks), 1)
        < lax.broadcasted_iota(jnp.int32, (toks, toks), 0)
    ).astype(F32).astype(BF16)
    place = jnp.dot(before, hit.astype(BF16), preferred_element_type=F32)
    chosen = jnp.where(place == place_of.astype(F32), hit, 0.0)
    sel_ref[...] = chosen.astype(BF16)
    is_x = core == 0
    scaled = jnp.where(is_x, chosen, chosen * weight).astype(BF16)

    for j in range(1, groups):
        landed(ra.at[(d + groups - j) % groups], ra_sem.at[j - 1])
    picked = lax.dot_general(
        scaled, ra[...].reshape(toks, qw), TN, preferred_element_type=F32
    ).astype(BF16)
    sb[...] = picked.reshape(experts, most, qw)
    rb[core, y, 0] = picked[0:most]

    def target_of(i, sign):
        k, dx = i // xs, i % xs
        dz = (k + 1) // 2 * (2 * (k % 2) - 1) * sign
        return (x + sign * dx + xs) % xs * zs + (z + dz + zs) % zs

    for g in range(parts):
        def send_rows(i, carry, g=g):
            remote(
                sb.at[i], rb.at[core, y, i], sb_sem.at[g], rb_sem.at[g],
                expert=target_of(i, 1),
            ).start()
            return carry

        lax.fori_loop(max(1, g * slots), (g + 1) * slots, send_rows, 0)

    first = [max(1, g * slots) for g in range(parts)]

    def part(g, low=0, high=None):
        low, high = g * slots + low, g * slots + (slots if high is None else high)
        return pl.ds(low, high - low)

    half = slots // 2
    pending = []

    def go(copy):
        copy.start()
        pending.append(copy)

    def stage_own(g):
        count = (g + 1) * slots - first[g]
        landed(rb.at[core, y, pl.ds(first[g], count)], rb_sem.at[g])
        mine = rb.at[core, y, part(g)]
        go(remote(mine, mine, sy_sem.at[g, 0], ry_sem.at[g, 0], dp=up))
        go(remote(mine, mine, sy_sem.at[g, 1], ry_sem.at[g, 1], dp=down))
        go(remote(mine, mine, sc_sem.at[g, 0], rc_sem.at[g, 0], dp=other))

    def stage_near(g):
        low = rb.at[core, down_y, part(g)]
        landed(low, ry_sem.at[g, 0])
        piece = rb.at[core, down_y, part(g, 0, half)]
        go(remote(piece, piece, sy_sem.at[g, 2], ry_sem.at[g, 2], dp=up))
        go(remote(low, low, sc_sem.at[g, 1], rc_sem.at[g, 1], dp=other))
        high = rb.at[core, up_y, part(g)]
        landed(high, ry_sem.at[g, 1])
        piece = rb.at[core, up_y, part(g, half)]
        go(remote(piece, piece, sy_sem.at[g, 3], ry_sem.at[g, 3], dp=down))
        go(remote(high, high, sc_sem.at[g, 2], rc_sem.at[g, 2], dp=other))

    def stage_far(g):
        landed(rb.at[core, far_y, part(g, 0, half)], ry_sem.at[g, 2])
        landed(rb.at[core, far_y, part(g, half)], ry_sem.at[g, 3])
        whole = rb.at[core, far_y, part(g)]
        go(remote(whole, whole, sc_sem.at[g, 3], rc_sem.at[g, 3], dp=other))

    def stage_compute(g):
        if g == 0:
            for load in loads:
                load.wait()
        for at, which in enumerate((y, down_y, up_y, far_y)):
            landed(rb.at[1 - core, which, part(g)], rc_sem.at[g, at])
        gu = jnp.zeros((rows, 2 * hid), F32)
        dh = jnp.zeros((rows, hid), F32)
        for q in range(QUARTERS):
            cols = slice(q * qw, (q + 1) * qw)
            gu += jnp.dot(
                rb[0, q, part(g)].reshape(rows, qw), wcat[cols, :], preferred_element_type=F32
            )
            dh += lax.dot_general(
                rb[1, q, part(g)].reshape(rows, qw), wd[:, cols], NT, preferred_element_type=F32
            )
        gate, upv = gu[:, 0:hid], gu[:, hid : 2 * hid]
        sig = jax.nn.sigmoid(gate)
        dgate = dh * upv * sig * (1.0 + gate * (1.0 - sig))
        dup = dh * gate * sig
        both = jnp.concatenate([dgate.astype(BF16), dup.astype(BF16)], axis=1)
        dd[g * rows : (g + 1) * rows, :] = both
        for q in range(QUARTERS):
            back = lax.dot_general(
                both, wcat[q * qw : (q + 1) * qw, :], NT, preferred_element_type=F32
            )
            left = back[:, 0:wide]
            right = back[:, wide:qw]
            if narrow < wide:
                right = jnp.concatenate([right, jnp.zeros((rows, wide - narrow), F32)], axis=1)
            keep[g, q] = jnp.where(is_x, left, right)
            sr1[g, q] = jnp.where(is_x, right, left).astype(BF16)
        go(remote(sr1.at[g], rr1.at[g], s1_sem.at[g], r1_sem.at[g], dp=other))

    def stage_chip(g):
        landed(rr1.at[g], r1_sem.at[g])
        for q in range(QUARTERS):
            sr2[g, q] = (keep[g, q] + rr1[g, q].astype(F32)).astype(BF16)
        for j in range(1, QUARTERS):
            to = (y + j) % QUARTERS
            go(remote(
                sr2.at[g, to], rr2.at[g, j - 1], s2_sem.at[g, j - 1], r2_sem.at[g, j - 1],
                dp=to * CORES + core,
            ))

    def stage_back(g):
        for j in range(1, QUARTERS):
            landed(rr2.at[g, j - 1], r2_sem.at[g, j - 1])
        total = keep[g, y] + rr1[g, y].astype(F32)
        for j in range(1, QUARTERS):
            total += rr2[g, j - 1].astype(F32)
        total = total.astype(BF16)
        sr3[part(g)] = total.reshape(slots, most, wide)
        if g == 0:
            rr3[0] = total[0:most]

        def send_back(i, carry):
            remote(
                sr3.at[i], rr3.at[i], s3_sem.at[g], r3_sem.at[g], expert=target_of(i, -1)
            ).start()
            return carry

        lax.fori_loop(first[g], (g + 1) * slots, send_back, 0)

    def weight_grads(q):
        grads = lax.dot_general(
            rb[0, q].reshape(experts * most, qw), dd[...], TN, preferred_element_type=F32
        )
        out_g[0, q * qw : (q + 1) * qw, :] = grads[:, 0:hid].astype(BF16)
        out_u[0, q * qw : (q + 1) * qw, :] = grads[:, hid : 2 * hid].astype(BF16)

    stages = (stage_own, stage_near, stage_far, stage_compute, stage_chip, stage_back)
    for step in range(parts + len(stages) - 1):
        for lag, stage in enumerate(stages):
            if 0 <= step - lag < parts:
                stage(step - lag)
        done = step - (parts - 1) - 3
        if done == 0:
            weight_grads(0)
        elif done == 1:
            weight_grads(1)
        elif done == 2:
            weight_grads(2)
            weight_grads(3)

    summed = jnp.zeros((toks, wide), F32)
    for g in range(parts):
        count = (g + 1) * slots - first[g]
        landed(rr3.at[pl.ds(first[g], count)], r3_sem.at[g])
        summed += jnp.dot(
            sel_ref[:, g * rows : (g + 1) * rows],
            rr3[part(g)].reshape(rows, wide),
            preferred_element_type=F32,
        )
    sf[...] = summed.astype(BF16).reshape(groups, per, wide)
    rf[d] = sf[d]
    for j in range(1, groups):
        p = (d + j) % groups
        go(remote(sf.at[p], rf.at[d], sf_sem.at[j - 1], rf_sem.at[j - 1], dp=p))
    for copy in sent_i + sent_a + pending[: -(groups - 1)]:
        copy.wait_send()
    for g in range(parts):
        count = (g + 1) * slots - first[g]
        landed(sb.at[pl.ds(first[g], count)], sb_sem.at[g])
        landed(sr3.at[pl.ds(first[g], count)], s3_sem.at[g])
    for j in range(1, groups):
        landed(rf.at[(d + groups - j) % groups], rf_sem.at[j - 1])
    for p in range(groups):
        at, size = p // CORES * qw + p % CORES * wide, (wide, narrow)[p % CORES]
        out_t[0, :, at : at + size] = rf[p, :, 0:size]
    for copy in pending[-(groups - 1) :]:
        copy.wait_send()


def on_device(z_size, tokens, grad_out, routes, gate_scores, w_gate, w_up, w_down):
    groups = lax.axis_size("dp")
    experts = lax.axis_size("expert")
    per, width = tokens.shape[1:]
    hid = w_gate.shape[2]
    toks = per * groups
    c = shape_of(experts, z_size, width, toks, routes.shape[2], hid)
    most, qw, wide, parts, slots = c["most"], c["qw"], c["wide"], c["parts"], c["slots"]
    rows = slots * most
    vmem = pl.BlockSpec(memory_space=pltpu.VMEM)
    hbm = pl.BlockSpec(memory_space=pl.ANY)
    dma = pltpu.SemaphoreType.DMA
    return pl.pallas_call(
        functools.partial(kernel, c),
        out_shape=(
            jax.ShapeDtypeStruct(tokens.shape, BF16),
            jax.ShapeDtypeStruct(w_gate.shape, BF16),
            jax.ShapeDtypeStruct(w_up.shape, BF16),
        ),
        in_specs=[vmem] * 4 + [hbm] * 3,
        out_specs=(vmem, vmem, vmem),
        scratch_shapes=[
            pltpu.VMEM((width, 2 * hid), BF16),
            pltpu.VMEM((hid, width), BF16),
            pltpu.VMEM((groups, per, qw), BF16),
            pltpu.VMEM((groups, per, qw), BF16),
            pltpu.VMEM((2, per, 128), F32),
            pltpu.VMEM((groups, 2, per, 128), F32),
            pltpu.VMEM((experts, most, qw), BF16),
            pltpu.VMEM((CORES, QUARTERS, experts, most, qw), BF16),
            pltpu.VMEM((experts * most, 2 * hid), BF16),
            pltpu.VMEM((parts, QUARTERS, rows, wide), F32),
            pltpu.VMEM((parts, QUARTERS, rows, wide), BF16),
            pltpu.VMEM((parts, QUARTERS, rows, wide), BF16),
            pltpu.VMEM((parts, QUARTERS, rows, wide), BF16),
            pltpu.VMEM((parts, QUARTERS - 1, rows, wide), BF16),
            pltpu.VMEM((experts, most, wide), BF16),
            pltpu.VMEM((experts, most, wide), BF16),
            pltpu.VMEM((groups, per, wide), BF16),
            pltpu.VMEM((groups, per, wide), BF16),
            pltpu.VMEM((toks, experts * most), BF16),
            dma((3,)),
            dma((groups - 1,)),
            dma((groups - 1,)),
            dma((groups - 1,)),
            dma((groups - 1,)),
            dma((parts,)),
            dma((parts,)),
            dma((parts, 4)),
            dma((parts, 4)),
            dma((parts, 4)),
            dma((parts, 4)),
            dma((parts,)),
            dma((parts,)),
            dma((parts, 3)),
            dma((parts, 3)),
            dma((parts,)),
            dma((parts,)),
            dma((groups - 1,)),
            dma((groups - 1,)),
        ],
        compiler_params=pltpu.CompilerParams(
            collective_id=0, has_side_effects=True, vmem_limit_bytes=48 * 1024 * 1024
        ),
        cost_estimate=pl.CostEstimate(
            flops=14 * experts * most * width * hid, bytes_accessed=10 * width * hid,
            transcendentals=experts * most * hid,
        ),
    )(tokens, grad_out, routes, gate_scores, w_gate, w_up, w_down)


def solution(mesh):
    placed = (
        P("expert", "dp", None),
        P("expert", "dp", None),
        P("expert", "dp", None),
        P("expert", "dp", None),
        P("expert", None, "dp"),
        P("expert", None, "dp"),
        P("expert", "dp", None),
    )
    z_size = 16 if mesh.shape["expert"] == 64 else 2
    return jax.shard_map(
        functools.partial(on_device, z_size),
        mesh=mesh,
        in_specs=placed,
        out_specs=(P("expert", "dp", None), P("expert", None, "dp"), P("expert", None, "dp")),
        check_vma=False,
    )
```

```python
import functools

import jax
import jax.numpy as jnp
from jax import lax
from jax.experimental import pallas as pl
from jax.experimental.pallas import tpu as pltpu
from jax.sharding import PartitionSpec as P

ROUTED = 256
CORES = 2
QUARTERS = 4
PARTS = 8
MESH = pl.DeviceIdType.MESH
F32, BF16 = jnp.float32, jnp.bfloat16
NT = (((1,), (1,)), ((), ()))
TN = (((0,), (0,)), ((), ()))


def order_of(z_size):
    steps = [0]
    for h in range(1, z_size // 2 + 1):
        steps += [h] if 2 * h == z_size else [h, -h]
    far = sorted(steps, key=lambda s: (-abs(s), -s))
    return far[::-1]


def shape_of(mesh_experts, columns_z, width, tok_col, top, hidden):
    z_size = columns_z
    x_size = mesh_experts // z_size
    most = max(2, 2 * tok_col * top // ROUTED)
    quarter = width // QUARTERS
    tiles = quarter // 128
    wide = (tiles + 1) // 2 * 128
    parts = min(PARTS, z_size)
    return dict(
        order=order_of(z_size), xs=x_size, zs=z_size, most=most, qw=quarter, wide=wide, parts=parts,
        slots=mesh_experts // parts, experts=mesh_experts, toks=tok_col, top=top, hid=hidden,
    )


def kernel(
    c, tok_hbm, dy_hbm, routes_hbm, scores_hbm, wg_hbm, wu_hbm, wd_hbm,
    out_t, out_g, out_u,
    wcat, wd, sa, ra, sb, rb, dd, keep, sr1, rr1, sr2, rr2, sr3, rr3, sf, rf, sel_ref,
    tok_ref, dy_ref, routes_ref, scores_ref, in_sem, w_sem, ring_sem, sa_sem, ra_sem, sb_sem, rb_sem,
    sy_sem, ry_sem, sc_sem, rc_sem, s1_sem, r1_sem, s2_sem, r2_sem, s3_sem, r3_sem,
    sf_sem, rf_sem,
):
    xs, zs, most, qw, wide, parts = c["xs"], c["zs"], c["most"], c["qw"], c["wide"], c["parts"]
    slots, experts, toks, hid = c["slots"], c["experts"], c["toks"], c["hid"]
    narrow = qw - wide
    order = c["order"]
    own_slot = order.index(0) * xs
    top = c["top"]
    rows = slots * most
    groups = CORES * QUARTERS
    per = toks // groups
    d = lax.axis_index("dp")
    e = lax.axis_index("expert")
    rem, div = lax.rem, lax.div
    y, core = div(d, CORES), rem(d, CORES)
    x, z = div(e, zs), rem(e, zs)
    other = y * CORES + (1 - core)
    up_y, down_y = rem(y + 1, QUARTERS), rem(y + QUARTERS - 1, QUARTERS)
    far_y = rem(y + 2, QUARTERS)
    up, down = up_y * CORES + core, down_y * CORES + core

    def remote(src, dst, send, recv, **where):
        return pltpu.make_async_remote_copy(
            src_ref=src, dst_ref=dst, send_sem=send, recv_sem=recv,
            device_id=where, device_id_type=MESH,
        )

    def landed(ref, sem):
        pltpu.make_async_copy(ref, ref, sem).wait()

    small = [
        pltpu.make_async_copy(src, dst, in_sem.at[i])
        for i, (src, dst) in enumerate((
            (routes_hbm, routes_ref), (scores_hbm, scores_ref),
            (tok_hbm, tok_ref), (dy_hbm, dy_ref),
        ))
    ]
    for load in small:
        load.start()
    loads = [
        pltpu.make_async_copy(wg_hbm.at[0], wcat.at[:, 0:hid], w_sem.at[0]),
        pltpu.make_async_copy(wu_hbm.at[0], wcat.at[:, hid : 2 * hid], w_sem.at[1]),
        pltpu.make_async_copy(wd_hbm.at[0], wd, w_sem.at[2]),
    ]
    for load in loads:
        load.start()

    barrier = pltpu.get_barrier_semaphore()
    for j in range(1, groups):
        pl.semaphore_signal(
            barrier, inc=1, device_id={"dp": rem(d + j, groups)}, device_id_type=MESH
        )

    for j in range(1, xs):
        pl.semaphore_signal(
            barrier, inc=1, device_id={"expert": rem(x + j, xs) * zs + z}, device_id_type=MESH
        )

    def greet(j, carry):
        pl.semaphore_signal(
            barrier, inc=1, device_id={"expert": x * zs + rem(z + j, zs)}, device_id_type=MESH
        )
        return carry

    lax.fori_loop(1, zs, greet, 0)

    for load in small:
        load.wait()
    for p in range(groups):
        source = tok_ref if p % CORES == 0 else dy_ref
        at = p // CORES * qw
        sa[p, :, 0:qw] = source[0, :, at : at + qw]
        sa[p, :, qw : qw + top] = routes_ref[0].astype(F32).astype(BF16)
        sa[p, :, qw + 128 : qw + 128 + top] = scores_ref[0]
    ra[d] = sa[d]
    pl.semaphore_wait(barrier, groups - 1 + xs - 1 + zs - 1)

    sent_a = []
    for j in range(1, groups):
        p = rem(d + j, groups)
        sent_a.append(remote(sa.at[p], ra.at[d], sa_sem.at[j - 1], ra_sem.at[j - 1], dp=p))
        sent_a[-1].start()
    for j in range(1, xs):
        pl.semaphore_signal(
            ring_sem, inc=1, device_id={"expert": rem(x + j, xs) * zs + z}, device_id_type=MESH
        )

    shape = (toks, experts * most)
    row = lax.broadcasted_iota(jnp.int32, shape, 1)
    place_of = row & (most - 1)
    slot_of = row >> (most.bit_length() - 1)
    dx_of = slot_of & (xs - 1)
    k_of = slot_of >> (xs.bit_length() - 1)
    dz_of = jnp.zeros(shape, jnp.int32)
    for k, dz in enumerate(order):
        dz_of = jnp.where(k_of == k, dz, dz_of)
    target = (((x + dx_of) & (xs - 1)) * zs + ((z + dz_of) & (zs - 1))).astype(F32)
    before = (
        lax.broadcasted_iota(jnp.int32, (toks, toks), 1)
        < lax.broadcasted_iota(jnp.int32, (toks, toks), 0)
    ).astype(F32).astype(BF16)
    for j in range(1, groups):
        landed(ra.at[rem(d + groups - j, groups)], ra_sem.at[j - 1])
    route = ra[:, :, qw : qw + 128].reshape(toks, 128).astype(F32)
    score = ra[:, :, qw + 128 : qw + 256].reshape(toks, 128).astype(F32)
    hit = jnp.zeros(shape, F32)
    weight = jnp.zeros(shape, F32)
    for k in range(c["top"]):
        same = route[:, k : k + 1] == target
        hit = jnp.where(same, 1.0, hit)
        weight = jnp.where(same, score[:, k : k + 1], weight)
    place = jnp.dot(before, hit.astype(BF16), preferred_element_type=F32)
    chosen = jnp.where(place == place_of.astype(F32), hit, 0.0)
    sel_ref[...] = chosen.astype(BF16)
    is_x = core == 0
    scaled = jnp.where(is_x, chosen, chosen * weight).astype(BF16)

    picked = lax.dot_general(
        scaled, ra[:, :, 0:qw].reshape(toks, qw), TN, preferred_element_type=F32
    ).astype(BF16)
    sb[...] = picked.reshape(experts, most, qw)
    rb[core, y, own_slot] = picked[own_slot * most : (own_slot + 1) * most]

    pl.semaphore_wait(ring_sem, xs - 1)
    def exchange(g, sign, src, dst, send, recv):
        for k in range(g * slots // xs, (g + 1) * slots // xs):
            to_z = rem(z + sign * order[k] + zs, zs)

            def send_rows(dx, carry, k=k, to_z=to_z):
                to = rem(x + sign * dx + xs, xs) * zs + to_z
                remote(
                    src.at[k * xs + dx], dst.at[k * xs + dx], send.at[g], recv.at[g], expert=to
                ).start()
                return carry

            lax.fori_loop(1 if order[k] == 0 else 0, xs, send_rows, 0)

    mine_rb = rb.at[core, y]
    for g in range(parts):
        exchange(g, 1, sb, mine_rb, sb_sem, rb_sem)

    def arrived(g, ref, sem):
        low, high = g * slots, (g + 1) * slots
        if low <= own_slot < high:
            if own_slot > low:
                landed(ref.at[pl.ds(low, own_slot - low)], sem)
            low = own_slot + 1
        landed(ref.at[pl.ds(low, high - low)], sem)

    def part(g, low=0, high=None):
        low, high = g * slots + low, g * slots + (slots if high is None else high)
        return pl.ds(low, high - low)

    half = slots // 2
    pending = []

    def go(copy):
        copy.start()
        pending.append(copy)

    def stage_own(g):
        arrived(g, mine_rb, rb_sem.at[g])
        mine = rb.at[core, y, part(g)]
        go(remote(mine, mine, sy_sem.at[g, 0], ry_sem.at[g, 0], dp=up))
        go(remote(mine, mine, sy_sem.at[g, 1], ry_sem.at[g, 1], dp=down))
        go(remote(mine, mine, sc_sem.at[g, 0], rc_sem.at[g, 0], dp=other))

    def stage_near(g):
        low = rb.at[core, down_y, part(g)]
        landed(low, ry_sem.at[g, 0])
        piece = rb.at[core, down_y, part(g, 0, half)]
        go(remote(piece, piece, sy_sem.at[g, 2], ry_sem.at[g, 2], dp=up))
        go(remote(low, low, sc_sem.at[g, 1], rc_sem.at[g, 1], dp=other))
        high = rb.at[core, up_y, part(g)]
        landed(high, ry_sem.at[g, 1])
        piece = rb.at[core, up_y, part(g, half)]
        go(remote(piece, piece, sy_sem.at[g, 3], ry_sem.at[g, 3], dp=down))
        go(remote(high, high, sc_sem.at[g, 2], rc_sem.at[g, 2], dp=other))

    def stage_far(g):
        landed(rb.at[core, far_y, part(g, 0, half)], ry_sem.at[g, 2])
        landed(rb.at[core, far_y, part(g, half)], ry_sem.at[g, 3])
        whole = rb.at[core, far_y, part(g)]
        go(remote(whole, whole, sc_sem.at[g, 3], rc_sem.at[g, 3], dp=other))

    def stage_compute(g):
        if g == 0:
            for load in loads:
                load.wait()
        for at, which in enumerate((y, down_y, up_y, far_y)):
            landed(rb.at[1 - core, which, part(g)], rc_sem.at[g, at])
        gu = jnp.zeros((rows, 2 * hid), F32)
        dh = jnp.zeros((rows, hid), F32)
        for q in range(QUARTERS):
            cols = slice(q * qw, (q + 1) * qw)
            gu += jnp.dot(
                rb[0, q, part(g)].reshape(rows, qw), wcat[cols, :], preferred_element_type=F32
            )
            dh += lax.dot_general(
                rb[1, q, part(g)].reshape(rows, qw), wd[:, cols], NT, preferred_element_type=F32
            )
        gate, upv = gu[:, 0:hid], gu[:, hid : 2 * hid]
        sig = jax.nn.sigmoid(gate)
        dgate = dh * upv * sig * (1.0 + gate * (1.0 - sig))
        dup = dh * gate * sig
        both = jnp.concatenate([dgate.astype(BF16), dup.astype(BF16)], axis=1)
        dd[g * rows : (g + 1) * rows, :] = both
        for q in range(QUARTERS):
            back = lax.dot_general(
                both, wcat[q * qw : (q + 1) * qw, :], NT, preferred_element_type=F32
            )
            left = back[:, 0:wide]
            right = back[:, wide:qw]
            if narrow < wide:
                right = jnp.concatenate([right, jnp.zeros((rows, wide - narrow), F32)], axis=1)
            keep[g, q] = jnp.where(is_x, left, right)
            sr1[g, q] = jnp.where(is_x, right, left).astype(BF16)
        go(remote(sr1.at[g], rr1.at[g], s1_sem.at[g], r1_sem.at[g], dp=other))

    def stage_chip(g):
        landed(rr1.at[g], r1_sem.at[g])
        for q in range(QUARTERS):
            sr2[g, q] = (keep[g, q] + rr1[g, q].astype(F32)).astype(BF16)
        for j in range(1, QUARTERS):
            to = rem(y + j, QUARTERS)
            go(remote(
                sr2.at[g, to], rr2.at[g, j - 1], s2_sem.at[g, j - 1], r2_sem.at[g, j - 1],
                dp=to * CORES + core,
            ))

    def stage_back(g):
        for j in range(1, QUARTERS):
            landed(rr2.at[g, j - 1], r2_sem.at[g, j - 1])
        total = keep[g, y] + rr1[g, y].astype(F32)
        for j in range(1, QUARTERS):
            total += rr2[g, j - 1].astype(F32)
        total = total.astype(BF16)
        sr3[part(g)] = total.reshape(slots, most, wide)
        if g * slots <= own_slot < (g + 1) * slots:
            at = (own_slot - g * slots) * most
            rr3[own_slot] = total[at : at + most]
        exchange(g, -1, sr3, rr3, s3_sem, r3_sem)

    def weight_grads(q):
        grads = lax.dot_general(
            rb[0, q].reshape(experts * most, qw), dd[...], TN, preferred_element_type=F32
        )
        out_g[0, q * qw : (q + 1) * qw, :] = grads[:, 0:hid].astype(BF16)
        out_u[0, q * qw : (q + 1) * qw, :] = grads[:, hid : 2 * hid].astype(BF16)

    stages = (stage_own, stage_near, stage_far, stage_compute, stage_chip, stage_back)
    for step in range(parts + len(stages) - 1):
        for lag, stage in enumerate(stages):
            if 0 <= step - lag < parts:
                stage(step - lag)
        done = step - (parts - 1) - 3
        if done == 0:
            weight_grads(0)
        elif done == 1:
            weight_grads(1)
        elif done == 2:
            weight_grads(2)
            weight_grads(3)

    summed = jnp.zeros((toks, wide), F32)
    for g in range(parts):
        arrived(g, rr3, r3_sem.at[g])
        summed += jnp.dot(
            sel_ref[:, g * rows : (g + 1) * rows],
            rr3[part(g)].reshape(rows, wide),
            preferred_element_type=F32,
        )
    sf[...] = summed.astype(BF16).reshape(groups, per, wide)
    rf[d] = sf[d]
    for j in range(1, groups):
        p = rem(d + j, groups)
        go(remote(sf.at[p], rf.at[d], sf_sem.at[j - 1], rf_sem.at[j - 1], dp=p))
    for copy in sent_a + pending[: -(groups - 1)]:
        copy.wait_send()
    for g in range(parts):
        arrived(g, sb, sb_sem.at[g])
        arrived(g, sr3, s3_sem.at[g])
    for j in range(1, groups):
        landed(rf.at[rem(d + groups - j, groups)], rf_sem.at[j - 1])
    for p in range(groups):
        at, size = p // CORES * qw + p % CORES * wide, (wide, narrow)[p % CORES]
        out_t[0, :, at : at + size] = rf[p, :, 0:size]
    for copy in pending[-(groups - 1) :]:
        copy.wait_send()


def on_device(z_size, tokens, grad_out, routes, gate_scores, w_gate, w_up, w_down):
    groups = lax.axis_size("dp")
    experts = lax.axis_size("expert")
    per, width = tokens.shape[1:]
    hid = w_gate.shape[2]
    toks = per * groups
    c = shape_of(experts, z_size, width, toks, routes.shape[2], hid)
    most, qw, wide, parts, slots = c["most"], c["qw"], c["wide"], c["parts"], c["slots"]
    rows = slots * most
    vmem = pl.BlockSpec(memory_space=pltpu.VMEM)
    hbm = pl.BlockSpec(memory_space=pl.ANY)
    dma = pltpu.SemaphoreType.DMA
    return pl.pallas_call(
        functools.partial(kernel, c),
        out_shape=(
            jax.ShapeDtypeStruct(tokens.shape, BF16),
            jax.ShapeDtypeStruct(w_gate.shape, BF16),
            jax.ShapeDtypeStruct(w_up.shape, BF16),
        ),
        in_specs=[hbm] * 7,
        out_specs=(vmem, vmem, vmem),
        scratch_shapes=[
            pltpu.VMEM((width, 2 * hid), BF16),
            pltpu.VMEM((hid, width), BF16),
            pltpu.VMEM((groups, per, qw + 256), BF16),
            pltpu.VMEM((groups, per, qw + 256), BF16),
            pltpu.VMEM((experts, most, qw), BF16),
            pltpu.VMEM((CORES, QUARTERS, experts, most, qw), BF16),
            pltpu.VMEM((experts * most, 2 * hid), BF16),
            pltpu.VMEM((parts, QUARTERS, rows, wide), F32),
            pltpu.VMEM((parts, QUARTERS, rows, wide), BF16),
            pltpu.VMEM((parts, QUARTERS, rows, wide), BF16),
            pltpu.VMEM((parts, QUARTERS, rows, wide), BF16),
            pltpu.VMEM((parts, QUARTERS - 1, rows, wide), BF16),
            pltpu.VMEM((experts, most, wide), BF16),
            pltpu.VMEM((experts, most, wide), BF16),
            pltpu.VMEM((groups, per, wide), BF16),
            pltpu.VMEM((groups, per, wide), BF16),
            pltpu.VMEM((toks, experts * most), BF16),
            pltpu.VMEM(tokens.shape, BF16),
            pltpu.VMEM(grad_out.shape, BF16),
            pltpu.VMEM(routes.shape, jnp.int32),
            pltpu.VMEM(gate_scores.shape, BF16),
            dma((4,)),
            dma((3,)),
            pltpu.SemaphoreType.REGULAR,
            dma((groups - 1,)),
            dma((groups - 1,)),
            dma((parts,)),
            dma((parts,)),
            dma((parts, 4)),
            dma((parts, 4)),
            dma((parts, 4)),
            dma((parts, 4)),
            dma((parts,)),
            dma((parts,)),
            dma((parts, 3)),
            dma((parts, 3)),
            dma((parts,)),
            dma((parts,)),
            dma((groups - 1,)),
            dma((groups - 1,)),
        ],
        compiler_params=pltpu.CompilerParams(
            collective_id=0, has_side_effects=True, vmem_limit_bytes=60 * 1024 * 1024
        ),
        cost_estimate=pl.CostEstimate(
            flops=14 * experts * most * width * hid, bytes_accessed=10 * width * hid,
            transcendentals=experts * most * hid,
        ),
    )(tokens, grad_out, routes, gate_scores, w_gate, w_up, w_down)


def solution(mesh):
    placed = (
        P("expert", "dp", None),
        P("expert", "dp", None),
        P("expert", "dp", None),
        P("expert", "dp", None),
        P("expert", None, "dp"),
        P("expert", None, "dp"),
        P("expert", "dp", None),
    )
    z_size = 16 if mesh.shape["expert"] == 64 else 2
    return jax.shard_map(
        functools.partial(on_device, z_size),
        mesh=mesh,
        in_specs=placed,
        out_specs=(P("expert", "dp", None), P("expert", None, "dp"), P("expert", None, "dp")),
        check_vma=False,
    )
```

```python
import functools

import jax
import jax.numpy as jnp
from jax import lax
from jax.experimental import pallas as pl
from jax.experimental.pallas import tpu as pltpu
from jax.sharding import PartitionSpec as P

ROUTED = 256
CORES = 2
QUARTERS = 4
SIZES = (2, 2, 2, 2, 2, 2, 2, 2)
RELAYED = 0
PLAN = (
    (0, 0), (0, 1), (0, 2), (1, 0), (0, 3), (2, 0), (1, 1), (3, 0),
    (2, 1), (0, 4), (1, 2), (3, 1), (2, 2), (1, 3), (0, 5), (3, 2),
    (2, 3), (4, 0), (3, 3), (1, 4), (0, 6), (2, 4), (4, 1), (3, 4),
    (1, 5), (0, 7), (2, 5), (4, 2), (4, 3), (3, 5), (1, 6), (2, 6),
    (4, 4), (3, 6), (1, 7), (2, 7), (4, 5), (4, 6), (3, 7), (4, 7),
)
MESH = pl.DeviceIdType.MESH
F32, BF16 = jnp.float32, jnp.bfloat16
NT = (((1,), (1,)), ((), ()))
TN = (((0,), (0,)), ((), ()))


def order_of(z_size):
    steps = [0]
    for h in range(1, z_size // 2 + 1):
        steps += [h] if 2 * h == z_size else [h, -h]
    far = sorted(steps, key=lambda s: (-abs(s), -s))
    return far[::-1]


def default_plan(parts):
    stages = (0, 1, 5, 2, 3, 4) if RELAYED else (0, 1, 2, 3, 4)
    return [(stage, g) for g in range(parts) for stage in stages]


def shape_of(mesh_experts, columns_z, width, tok_col, top, hidden):
    z_size = columns_z
    x_size = mesh_experts // z_size
    most = max(2, 2 * tok_col * top // ROUTED)
    quarter = width // QUARTERS
    tiles = quarter // 128
    wide = (tiles + 1) // 2 * 128
    sizes = SIZES if sum(SIZES) == z_size else (1,) * z_size
    starts = [sum(sizes[:g]) * x_size for g in range(len(sizes) + 1)]
    return dict(
        order=order_of(z_size), xs=x_size, zs=z_size, most=most, qw=quarter, wide=wide, starts=starts,
        experts=mesh_experts, toks=tok_col, top=top, hid=hidden,
    )


def kernel(
    c, tok_hbm, dy_hbm, routes_hbm, scores_hbm, wg_hbm, wu_hbm, wd_hbm,
    out_t, out_g, out_u,
    wcat, wd, sa, ra, sb, rb, dd, keep, sr1, rr1, sr2, rr2, sr3, rr3, sf, rf, sel_ref,
    tok_ref, dy_ref, routes_ref, scores_ref, in_sem, w_sem, ring_sem, sa_sem, ra_sem, sb_sem, rb_sem,
    sy_sem, ry_sem, sc_sem, rc_sem, s1_sem, r1_sem, s2_sem, r2_sem, s3_sem, r3_sem,
    sf_sem, rf_sem,
):
    xs, zs, most, qw, wide, starts = c["xs"], c["zs"], c["most"], c["qw"], c["wide"], c["starts"]
    experts, toks, hid = c["experts"], c["toks"], c["hid"]
    parts = len(starts) - 1
    narrow = qw - wide
    order = c["order"]
    own_slot = order.index(0) * xs
    top = c["top"]
    groups = CORES * QUARTERS
    per = toks // groups
    d = lax.axis_index("dp")
    e = lax.axis_index("expert")
    rem, div = lax.rem, lax.div
    y, core = div(d, CORES), rem(d, CORES)
    x, z = div(e, zs), rem(e, zs)
    other = y * CORES + (1 - core)
    up_y, down_y = rem(y + 1, QUARTERS), rem(y + QUARTERS - 1, QUARTERS)
    far_y = rem(y + 2, QUARTERS)
    up, down = up_y * CORES + core, down_y * CORES + core

    def remote(src, dst, send, recv, **where):
        return pltpu.make_async_remote_copy(
            src_ref=src, dst_ref=dst, send_sem=send, recv_sem=recv,
            device_id=where, device_id_type=MESH,
        )

    def landed(ref, sem):
        pltpu.make_async_copy(ref, ref, sem).wait()

    small = [
        pltpu.make_async_copy(src, dst, in_sem.at[i])
        for i, (src, dst) in enumerate((
            (routes_hbm, routes_ref), (scores_hbm, scores_ref),
            (tok_hbm, tok_ref), (dy_hbm, dy_ref),
        ))
    ]
    for load in small:
        load.start()
    loads = [
        pltpu.make_async_copy(wg_hbm.at[0], wcat.at[:, 0:hid], w_sem.at[0]),
        pltpu.make_async_copy(wu_hbm.at[0], wcat.at[:, hid : 2 * hid], w_sem.at[1]),
        pltpu.make_async_copy(wd_hbm.at[0], wd, w_sem.at[2]),
    ]
    for load in loads:
        load.start()

    barrier = pltpu.get_barrier_semaphore()
    for j in range(1, groups):
        pl.semaphore_signal(
            barrier, inc=1, device_id={"dp": rem(d + j, groups)}, device_id_type=MESH
        )

    for j in range(1, xs):
        pl.semaphore_signal(
            barrier, inc=1, device_id={"expert": rem(x + j, xs) * zs + z}, device_id_type=MESH
        )

    def greet(j, carry):
        pl.semaphore_signal(
            barrier, inc=1, device_id={"expert": x * zs + rem(z + j, zs)}, device_id_type=MESH
        )
        return carry

    lax.fori_loop(1, zs, greet, 0)

    for load in small:
        load.wait()
    for p in range(groups):
        source = tok_ref if p % CORES == 0 else dy_ref
        at = p // CORES * qw
        sa[p, :, 0:qw] = source[0, :, at : at + qw]
        sa[p, :, qw : qw + top] = routes_ref[0].astype(F32).astype(BF16)
        sa[p, :, qw + 128 : qw + 128 + top] = scores_ref[0]
    ra[d] = sa[d]
    pl.semaphore_wait(barrier, groups - 1 + xs - 1 + zs - 1)

    sent_a = []
    for j in range(1, groups):
        p = rem(d + j, groups)
        sent_a.append(remote(sa.at[p], ra.at[d], sa_sem.at[j - 1], ra_sem.at[j - 1], dp=p))
        sent_a[-1].start()
    for j in range(1, xs):
        pl.semaphore_signal(
            ring_sem, inc=1, device_id={"expert": rem(x + j, xs) * zs + z}, device_id_type=MESH
        )

    shape = (toks, experts * most)
    row = lax.broadcasted_iota(jnp.int32, shape, 1)
    place_of = row & (most - 1)
    slot_of = row >> (most.bit_length() - 1)
    dx_of = slot_of & (xs - 1)
    k_of = slot_of >> (xs.bit_length() - 1)
    dz_of = jnp.zeros(shape, jnp.int32)
    for k, dz in enumerate(order):
        dz_of = jnp.where(k_of == k, dz, dz_of)
    target = (((x + dx_of) & (xs - 1)) * zs + ((z + dz_of) & (zs - 1))).astype(F32)
    before = (
        lax.broadcasted_iota(jnp.int32, (toks, toks), 1)
        < lax.broadcasted_iota(jnp.int32, (toks, toks), 0)
    ).astype(F32).astype(BF16)
    for j in range(1, groups):
        landed(ra.at[rem(d + groups - j, groups)], ra_sem.at[j - 1])
    route = ra[:, :, qw : qw + 128].reshape(toks, 128).astype(F32)
    score = ra[:, :, qw + 128 : qw + 256].reshape(toks, 128).astype(F32)
    hit = jnp.zeros(shape, F32)
    weight = jnp.zeros(shape, F32)
    for k in range(c["top"]):
        same = route[:, k : k + 1] == target
        hit = jnp.where(same, 1.0, hit)
        weight = jnp.where(same, score[:, k : k + 1], weight)
    place = jnp.dot(before, hit.astype(BF16), preferred_element_type=F32)
    chosen = jnp.where(place == place_of.astype(F32), hit, 0.0)
    sel_ref[...] = chosen.astype(BF16)
    is_x = core == 0
    scaled = jnp.where(is_x, chosen, chosen * weight).astype(BF16)

    picked = lax.dot_general(
        scaled, ra[:, :, 0:qw].reshape(toks, qw), TN, preferred_element_type=F32
    ).astype(BF16)
    sb[...] = picked.reshape(experts, most, qw)
    rb[core, y, own_slot] = picked[own_slot * most : (own_slot + 1) * most]

    pl.semaphore_wait(ring_sem, xs - 1)
    def exchange(g, sign, src, dst, send, recv):
        for k in range(starts[g] // xs, starts[g + 1] // xs):
            to_z = rem(z + sign * order[k] + zs, zs)

            def send_rows(dx, carry, k=k, to_z=to_z):
                to = rem(x + sign * dx + xs, xs) * zs + to_z
                remote(
                    src.at[k * xs + dx], dst.at[k * xs + dx], send.at[g], recv.at[g], expert=to
                ).start()
                return carry

            lax.fori_loop(1 if order[k] == 0 else 0, xs, send_rows, 0)

    mine_rb = rb.at[core, y]
    for g in range(parts):
        exchange(g, 1, sb, mine_rb, sb_sem, rb_sem)

    def arrived(g, ref, sem):
        low, high = starts[g], starts[g + 1]
        if low <= own_slot < high:
            if own_slot > low:
                landed(ref.at[pl.ds(low, own_slot - low)], sem)
            low = own_slot + 1
        landed(ref.at[pl.ds(low, high - low)], sem)

    def part(g, piece=None):
        low, high = starts[g], starts[g + 1]
        middle = (low + high) // 2
        if piece is not None:
            low, high = (low, middle) if piece == 0 else (middle, high)
        return pl.ds(low, high - low)

    def rows_of(g):
        return pl.ds(starts[g] * most, (starts[g + 1] - starts[g]) * most)

    pending = []

    def go(copy):
        copy.start()
        pending.append(copy)

    def stage_own(g):
        arrived(g, mine_rb, rb_sem.at[g])
        mine = rb.at[core, y, part(g)]
        go(remote(mine, mine, sy_sem.at[g, 0], ry_sem.at[g, 0], dp=up))
        go(remote(mine, mine, sy_sem.at[g, 1], ry_sem.at[g, 1], dp=down))
        if g >= RELAYED:
            go(remote(mine, mine, sy_sem.at[g, 2], ry_sem.at[g, 2], dp=far_y * CORES + core))
        go(remote(mine, mine, sc_sem.at[g, 0], rc_sem.at[g, 0], dp=other))

    def stage_near(g):
        low = rb.at[core, down_y, part(g)]
        landed(low, ry_sem.at[g, 0])
        if g < RELAYED:
            piece = rb.at[core, down_y, part(g, 0)]
            go(remote(piece, piece, sy_sem.at[g, 2], ry_sem.at[g, 2], dp=up))
        go(remote(low, low, sc_sem.at[g, 1], rc_sem.at[g, 1], dp=other))
        high = rb.at[core, up_y, part(g)]
        landed(high, ry_sem.at[g, 1])
        if g < RELAYED:
            piece = rb.at[core, up_y, part(g, 1)]
            go(remote(piece, piece, sy_sem.at[g, 3], ry_sem.at[g, 3], dp=down))
        go(remote(high, high, sc_sem.at[g, 2], rc_sem.at[g, 2], dp=other))
        if g >= RELAYED:
            stage_far(g)

    def stage_far(g):
        whole = rb.at[core, far_y, part(g)]
        if g < RELAYED:
            landed(rb.at[core, far_y, part(g, 0)], ry_sem.at[g, 2])
            landed(rb.at[core, far_y, part(g, 1)], ry_sem.at[g, 3])
        else:
            landed(whole, ry_sem.at[g, 2])
        go(remote(whole, whole, sc_sem.at[g, 3], rc_sem.at[g, 3], dp=other))

    def stage_compute(g):
        if g == 0:
            for load in loads:
                load.wait()
        for at, which in enumerate((y, down_y, up_y, far_y)):
            landed(rb.at[1 - core, which, part(g)], rc_sem.at[g, at])
        mine = rows_of(g)
        rows = mine.size
        gu = jnp.zeros((rows, 2 * hid), F32)
        dh = jnp.zeros((rows, hid), F32)
        for q in range(QUARTERS):
            cols = slice(q * qw, (q + 1) * qw)
            gu += jnp.dot(
                rb[0, q, part(g)].reshape(rows, qw), wcat[cols, :], preferred_element_type=F32
            )
            dh += lax.dot_general(
                rb[1, q, part(g)].reshape(rows, qw), wd[:, cols], NT, preferred_element_type=F32
            )
        gate, upv = gu[:, 0:hid], gu[:, hid : 2 * hid]
        sig = jax.nn.sigmoid(gate)
        dgate = dh * upv * sig * (1.0 + gate * (1.0 - sig))
        dup = dh * gate * sig
        both = jnp.concatenate([dgate.astype(BF16), dup.astype(BF16)], axis=1)
        dd[mine, :] = both
        for q in range(QUARTERS):
            back = lax.dot_general(
                both, wcat[q * qw : (q + 1) * qw, :], NT, preferred_element_type=F32
            )
            left = back[:, 0:wide]
            right = back[:, wide:qw]
            if narrow < wide:
                right = jnp.concatenate([right, jnp.zeros((rows, wide - narrow), F32)], axis=1)
            keep[q, mine] = jnp.where(is_x, left, right)
            sr1[q, mine] = jnp.where(is_x, right, left).astype(BF16)
        go(remote(sr1.at[:, mine], rr1.at[:, mine], s1_sem.at[g], r1_sem.at[g], dp=other))

    def stage_chip(g):
        mine = rows_of(g)
        landed(rr1.at[:, mine], r1_sem.at[g])
        for q in range(QUARTERS):
            sr2[q, mine] = (keep[q, mine] + rr1[q, mine].astype(F32)).astype(BF16)
        for j in range(1, QUARTERS):
            to = rem(y + j, QUARTERS)
            go(remote(
                sr2.at[to, mine], rr2.at[j - 1, mine], s2_sem.at[g, j - 1], r2_sem.at[g, j - 1],
                dp=to * CORES + core,
            ))

    def stage_back(g):
        mine = rows_of(g)
        for j in range(1, QUARTERS):
            landed(rr2.at[j - 1, mine], r2_sem.at[g, j - 1])
        total = keep[y, mine] + rr1[y, mine].astype(F32)
        for j in range(1, QUARTERS):
            total += rr2[j - 1, mine].astype(F32)
        total = total.astype(BF16)
        sr3[part(g)] = total.reshape(mine.size // most, most, wide)
        if starts[g] <= own_slot < starts[g + 1]:
            at = (own_slot - starts[g]) * most
            rr3[own_slot] = total[at : at + most]
        exchange(g, -1, sr3, rr3, s3_sem, r3_sem)

    def weight_grads(q):
        grads = lax.dot_general(
            rb[0, q].reshape(experts * most, qw), dd[...], TN, preferred_element_type=F32
        )
        out_g[0, q * qw : (q + 1) * qw, :] = grads[:, 0:hid].astype(BF16)
        out_u[0, q * qw : (q + 1) * qw, :] = grads[:, hid : 2 * hid].astype(BF16)

    def stages_of(g):
        tail = [stage_compute, stage_chip, stage_back]
        return [stage_own, stage_near] + ([stage_far] if g < RELAYED else []) + tail

    for stage, g in PLAN if parts == len(SIZES) else default_plan(parts):
        (stage_own, stage_near, stage_compute, stage_chip, stage_back, stage_far)[stage](g)
        if stage == 2 and g == parts - 1:
            weight_grads(0)
        if stage == 3 and g == parts - 1:
            weight_grads(1)
    weight_grads(2)
    weight_grads(3)

    for copy in sent_a + pending:
        copy.wait_send()
    for g in range(parts):
        arrived(g, sb, sb_sem.at[g])

    summed = jnp.zeros((toks, wide), F32)
    for g in range(parts):
        arrived(g, rr3, r3_sem.at[g])
        summed += jnp.dot(
            sel_ref[:, starts[g] * most : starts[g + 1] * most],
            rr3[part(g)].reshape(rows_of(g).size, wide),
            preferred_element_type=F32,
        )
    sf[...] = summed.astype(BF16).reshape(groups, per, wide)
    rf[d] = sf[d]
    for j in range(1, groups):
        p = rem(d + j, groups)
        go(remote(sf.at[p], rf.at[d], sf_sem.at[j - 1], rf_sem.at[j - 1], dp=p))
    for g in range(parts):
        arrived(g, sr3, s3_sem.at[g])
    for j in range(1, groups):
        landed(rf.at[rem(d + groups - j, groups)], rf_sem.at[j - 1])
    for p in range(groups):
        at, size = p // CORES * qw + p % CORES * wide, (wide, narrow)[p % CORES]
        out_t[0, :, at : at + size] = rf[p, :, 0:size]
    for copy in pending[-(groups - 1) :]:
        copy.wait_send()


def on_device(z_size, tokens, grad_out, routes, gate_scores, w_gate, w_up, w_down):
    groups = lax.axis_size("dp")
    experts = lax.axis_size("expert")
    per, width = tokens.shape[1:]
    hid = w_gate.shape[2]
    toks = per * groups
    c = shape_of(experts, z_size, width, toks, routes.shape[2], hid)
    most, qw, wide, parts = c["most"], c["qw"], c["wide"], len(c["starts"]) - 1
    rows = experts * most
    vmem = pl.BlockSpec(memory_space=pltpu.VMEM)
    hbm = pl.BlockSpec(memory_space=pl.ANY)
    dma = pltpu.SemaphoreType.DMA
    return pl.pallas_call(
        functools.partial(kernel, c),
        out_shape=(
            jax.ShapeDtypeStruct(tokens.shape, BF16),
            jax.ShapeDtypeStruct(w_gate.shape, BF16),
            jax.ShapeDtypeStruct(w_up.shape, BF16),
        ),
        in_specs=[hbm] * 7,
        out_specs=(vmem, vmem, vmem),
        scratch_shapes=[
            pltpu.VMEM((width, 2 * hid), BF16),
            pltpu.VMEM((hid, width), BF16),
            pltpu.VMEM((groups, per, qw + 256), BF16),
            pltpu.VMEM((groups, per, qw + 256), BF16),
            pltpu.VMEM((experts, most, qw), BF16),
            pltpu.VMEM((CORES, QUARTERS, experts, most, qw), BF16),
            pltpu.VMEM((experts * most, 2 * hid), BF16),
            pltpu.VMEM((QUARTERS, rows, wide), F32),
            pltpu.VMEM((QUARTERS, rows, wide), BF16),
            pltpu.VMEM((QUARTERS, rows, wide), BF16),
            pltpu.VMEM((QUARTERS, rows, wide), BF16),
            pltpu.VMEM((QUARTERS - 1, rows, wide), BF16),
            pltpu.VMEM((experts, most, wide), BF16),
            pltpu.VMEM((experts, most, wide), BF16),
            pltpu.VMEM((groups, per, wide), BF16),
            pltpu.VMEM((groups, per, wide), BF16),
            pltpu.VMEM((toks, experts * most), BF16),
            pltpu.VMEM(tokens.shape, BF16),
            pltpu.VMEM(grad_out.shape, BF16),
            pltpu.VMEM(routes.shape, jnp.int32),
            pltpu.VMEM(gate_scores.shape, BF16),
            dma((4,)),
            dma((3,)),
            pltpu.SemaphoreType.REGULAR,
            dma((groups - 1,)),
            dma((groups - 1,)),
            dma((parts,)),
            dma((parts,)),
            dma((parts, 4)),
            dma((parts, 4)),
            dma((parts, 4)),
            dma((parts, 4)),
            dma((parts,)),
            dma((parts,)),
            dma((parts, 3)),
            dma((parts, 3)),
            dma((parts,)),
            dma((parts,)),
            dma((groups - 1,)),
            dma((groups - 1,)),
        ],
        compiler_params=pltpu.CompilerParams(
            collective_id=0, has_side_effects=True, vmem_limit_bytes=60 * 1024 * 1024
        ),
        cost_estimate=pl.CostEstimate(
            flops=14 * experts * most * width * hid, bytes_accessed=10 * width * hid,
            transcendentals=experts * most * hid,
        ),
    )(tokens, grad_out, routes, gate_scores, w_gate, w_up, w_down)


def solution(mesh):
    placed = (
        P("expert", "dp", None),
        P("expert", "dp", None),
        P("expert", "dp", None),
        P("expert", "dp", None),
        P("expert", None, "dp"),
        P("expert", None, "dp"),
        P("expert", "dp", None),
    )
    z_size = 16 if mesh.shape["expert"] == 64 else 2
    return jax.shard_map(
        functools.partial(on_device, z_size),
        mesh=mesh,
        in_specs=placed,
        out_specs=(P("expert", "dp", None), P("expert", None, "dp"), P("expert", None, "dp")),
        check_vma=False,
    )
```

```python
import functools

import jax
import jax.numpy as jnp
from jax import lax
from jax.experimental import pallas as pl
from jax.experimental.pallas import tpu as pltpu
from jax.sharding import PartitionSpec as P

ROUTED = 256
CORES = 2
QUARTERS = 4
SIZES = (3, 3, 3, 3, 2, 2)
RELAYED = 0
PLAN = (
    (0, 0), (0, 1), (1, 0), (0, 2), (2, 0), (1, 1), (3, 0), (2, 1),
    (0, 3), (1, 2), (3, 1), (2, 2), (4, 0), (0, 4), (3, 2), (1, 3),
    (2, 3), (4, 1), (0, 5), (3, 3), (1, 4), (2, 4), (4, 2), (3, 4),
    (1, 5), (2, 5), (4, 3), (3, 5), (4, 4), (4, 5),
)
MESH = pl.DeviceIdType.MESH
F32, BF16 = jnp.float32, jnp.bfloat16
NT = (((1,), (1,)), ((), ()))
TN = (((0,), (0,)), ((), ()))


def order_of(z_size):
    steps = [0]
    for h in range(1, z_size // 2 + 1):
        steps += [h] if 2 * h == z_size else [h, -h]
    far = sorted(steps, key=lambda s: (-abs(s), -s))
    return far[::-1]


def default_plan(parts):
    stages = (0, 1, 5, 2, 3, 4) if RELAYED else (0, 1, 2, 3, 4)
    return [(stage, g) for g in range(parts) for stage in stages]


def shape_of(mesh_experts, columns_z, width, tok_col, top, hidden):
    z_size = columns_z
    x_size = mesh_experts // z_size
    most = max(2, 2 * tok_col * top // ROUTED)
    quarter = width // QUARTERS
    tiles = quarter // 128
    wide = (tiles + 1) // 2 * 128
    sizes = SIZES if sum(SIZES) == z_size else (1,) * z_size
    starts = [sum(sizes[:g]) * x_size for g in range(len(sizes) + 1)]
    return dict(
        order=order_of(z_size), xs=x_size, zs=z_size, most=most, qw=quarter, wide=wide, starts=starts,
        experts=mesh_experts, toks=tok_col, top=top, hid=hidden,
    )


def kernel(
    c, tok_hbm, dy_hbm, routes_hbm, scores_hbm, wg_hbm, wu_hbm, wd_hbm,
    out_t, out_g, out_u,
    wcat, wd, wt, wdt, sa, ra, sb, rb, dd, keep, sr1, rr1, sr2, rr2, sr3, rr3, sf, rf, sel_ref,
    tok_ref, dy_ref, routes_ref, scores_ref, in_sem, w_sem, ring_sem, sa_sem, ra_sem, sb_sem, rb_sem,
    sy_sem, ry_sem, sc_sem, rc_sem, s1_sem, r1_sem, s2_sem, r2_sem, s3_sem, r3_sem,
    sf_sem, rf_sem,
):
    xs, zs, most, qw, wide, starts = c["xs"], c["zs"], c["most"], c["qw"], c["wide"], c["starts"]
    experts, toks, hid = c["experts"], c["toks"], c["hid"]
    parts = len(starts) - 1
    narrow = qw - wide
    order = c["order"]
    own_slot = order.index(0) * xs
    top = c["top"]
    groups = CORES * QUARTERS
    per = toks // groups
    d = lax.axis_index("dp")
    e = lax.axis_index("expert")
    rem, div = lax.rem, lax.div
    y, core = div(d, CORES), rem(d, CORES)
    x, z = div(e, zs), rem(e, zs)
    other = y * CORES + (1 - core)
    up_y, down_y = rem(y + 1, QUARTERS), rem(y + QUARTERS - 1, QUARTERS)
    far_y = rem(y + 2, QUARTERS)
    up, down = up_y * CORES + core, down_y * CORES + core

    def remote(src, dst, send, recv, **where):
        return pltpu.make_async_remote_copy(
            src_ref=src, dst_ref=dst, send_sem=send, recv_sem=recv,
            device_id=where, device_id_type=MESH,
        )

    def landed(ref, sem):
        pltpu.make_async_copy(ref, ref, sem).wait()

    small = [
        pltpu.make_async_copy(src, dst, in_sem.at[i])
        for i, (src, dst) in enumerate((
            (routes_hbm, routes_ref), (scores_hbm, scores_ref),
            (tok_hbm, tok_ref), (dy_hbm, dy_ref),
        ))
    ]
    for load in small:
        load.start()
    loads = [
        pltpu.make_async_copy(wg_hbm.at[0], wcat.at[:, 0:hid], w_sem.at[0]),
        pltpu.make_async_copy(wu_hbm.at[0], wcat.at[:, hid : 2 * hid], w_sem.at[1]),
        pltpu.make_async_copy(wd_hbm.at[0], wd, w_sem.at[2]),
    ]
    for load in loads:
        load.start()

    barrier = pltpu.get_barrier_semaphore()
    for j in range(1, groups):
        pl.semaphore_signal(
            barrier, inc=1, device_id={"dp": rem(d + j, groups)}, device_id_type=MESH
        )

    for j in range(1, xs):
        pl.semaphore_signal(
            barrier, inc=1, device_id={"expert": rem(x + j, xs) * zs + z}, device_id_type=MESH
        )

    def greet(j, carry):
        pl.semaphore_signal(
            barrier, inc=1, device_id={"expert": x * zs + rem(z + j, zs)}, device_id_type=MESH
        )
        return carry

    lax.fori_loop(1, zs, greet, 0)

    for load in small:
        load.wait()
    for p in range(groups):
        source = tok_ref if p % CORES == 0 else dy_ref
        at = p // CORES * qw
        sa[p, :, 0:qw] = source[0, :, at : at + qw]
        sa[p, :, qw : qw + top] = routes_ref[0].astype(F32).astype(BF16)
        sa[p, :, qw + 128 : qw + 128 + top] = scores_ref[0]
    ra[d] = sa[d]
    pl.semaphore_wait(barrier, groups - 1 + xs - 1 + zs - 1)

    sent_a = []
    for j in range(1, groups):
        p = rem(d + j, groups)
        sent_a.append(remote(sa.at[p], ra.at[d], sa_sem.at[j - 1], ra_sem.at[j - 1], dp=p))
        sent_a[-1].start()
    for j in range(1, xs):
        pl.semaphore_signal(
            ring_sem, inc=1, device_id={"expert": rem(x + j, xs) * zs + z}, device_id_type=MESH
        )

    shape = (toks, experts * most)
    row = lax.broadcasted_iota(jnp.int32, shape, 1)
    place_of = row & (most - 1)
    slot_of = row >> (most.bit_length() - 1)
    dx_of = slot_of & (xs - 1)
    k_of = slot_of >> (xs.bit_length() - 1)
    dz_of = jnp.zeros(shape, jnp.int32)
    for k, dz in enumerate(order):
        dz_of = jnp.where(k_of == k, dz, dz_of)
    target = (((x + dx_of) & (xs - 1)) * zs + ((z + dz_of) & (zs - 1))).astype(F32)
    before = (
        lax.broadcasted_iota(jnp.int32, (toks, toks), 1)
        < lax.broadcasted_iota(jnp.int32, (toks, toks), 0)
    ).astype(F32).astype(BF16)
    for j in range(1, groups):
        landed(ra.at[rem(d + groups - j, groups)], ra_sem.at[j - 1])
    route = ra[:, :, qw : qw + 128].reshape(toks, 128).astype(F32)
    score = ra[:, :, qw + 128 : qw + 256].reshape(toks, 128).astype(F32)
    hit = jnp.zeros(shape, F32)
    weight = jnp.zeros(shape, F32)
    for k in range(c["top"]):
        same = route[:, k : k + 1] == target
        hit = jnp.where(same, 1.0, hit)
        weight = jnp.where(same, score[:, k : k + 1], weight)
    place = jnp.dot(before, hit.astype(BF16), preferred_element_type=F32)
    chosen = jnp.where(place == place_of.astype(F32), hit, 0.0)
    sel_ref[...] = chosen.astype(BF16)
    is_x = core == 0
    scaled = jnp.where(is_x, chosen, chosen * weight).astype(BF16)

    picked = lax.dot_general(
        scaled, ra[:, :, 0:qw].reshape(toks, qw), TN, preferred_element_type=F32
    ).astype(BF16)
    sb[...] = picked.reshape(experts, most, qw)
    rb[core, y, own_slot] = picked[own_slot * most : (own_slot + 1) * most]

    pl.semaphore_wait(ring_sem, xs - 1)
    def exchange(g, sign, src, dst, send, recv):
        for k in range(starts[g] // xs, starts[g + 1] // xs):
            to_z = rem(z + sign * order[k] + zs, zs)

            def send_rows(dx, carry, k=k, to_z=to_z):
                to = rem(x + sign * dx + xs, xs) * zs + to_z
                remote(
                    src.at[k * xs + dx], dst.at[k * xs + dx], send.at[g], recv.at[g], expert=to
                ).start()
                return carry

            lax.fori_loop(1 if order[k] == 0 else 0, xs, send_rows, 0)

    mine_rb = rb.at[core, y]
    for g in range(parts):
        exchange(g, 1, sb, mine_rb, sb_sem, rb_sem)

    def arrived(g, ref, sem):
        low, high = starts[g], starts[g + 1]
        if low <= own_slot < high:
            if own_slot > low:
                landed(ref.at[pl.ds(low, own_slot - low)], sem)
            low = own_slot + 1
        landed(ref.at[pl.ds(low, high - low)], sem)

    def part(g, piece=None):
        low, high = starts[g], starts[g + 1]
        middle = (low + high) // 2
        if piece is not None:
            low, high = (low, middle) if piece == 0 else (middle, high)
        return pl.ds(low, high - low)

    def rows_of(g):
        return pl.ds(starts[g] * most, (starts[g + 1] - starts[g]) * most)

    for load in loads:
        load.wait()
    for q in range(QUARTERS):
        cols = slice(q * qw, (q + 1) * qw)
        wt[:, cols] = wcat[cols, :].T
        wdt[cols, :] = wd[:, cols].T
    pending = []

    def go(copy):
        copy.start()
        pending.append(copy)

    def stage_own(g):
        arrived(g, mine_rb, rb_sem.at[g])
        mine = rb.at[core, y, part(g)]
        go(remote(mine, mine, sy_sem.at[g, 0], ry_sem.at[g, 0], dp=up))
        go(remote(mine, mine, sy_sem.at[g, 1], ry_sem.at[g, 1], dp=down))
        if g >= RELAYED:
            go(remote(mine, mine, sy_sem.at[g, 2], ry_sem.at[g, 2], dp=far_y * CORES + core))
        go(remote(mine, mine, sc_sem.at[g, 0], rc_sem.at[g, 0], dp=other))

    def stage_near(g):
        low = rb.at[core, down_y, part(g)]
        landed(low, ry_sem.at[g, 0])
        if g < RELAYED:
            piece = rb.at[core, down_y, part(g, 0)]
            go(remote(piece, piece, sy_sem.at[g, 2], ry_sem.at[g, 2], dp=up))
        go(remote(low, low, sc_sem.at[g, 1], rc_sem.at[g, 1], dp=other))
        high = rb.at[core, up_y, part(g)]
        landed(high, ry_sem.at[g, 1])
        if g < RELAYED:
            piece = rb.at[core, up_y, part(g, 1)]
            go(remote(piece, piece, sy_sem.at[g, 3], ry_sem.at[g, 3], dp=down))
        go(remote(high, high, sc_sem.at[g, 2], rc_sem.at[g, 2], dp=other))
        if g >= RELAYED:
            stage_far(g)

    def stage_far(g):
        whole = rb.at[core, far_y, part(g)]
        if g < RELAYED:
            landed(rb.at[core, far_y, part(g, 0)], ry_sem.at[g, 2])
            landed(rb.at[core, far_y, part(g, 1)], ry_sem.at[g, 3])
        else:
            landed(whole, ry_sem.at[g, 2])
        go(remote(whole, whole, sc_sem.at[g, 3], rc_sem.at[g, 3], dp=other))

    def stage_compute(g):
        for at, which in enumerate((y, down_y, up_y, far_y)):
            landed(rb.at[1 - core, which, part(g)], rc_sem.at[g, at])
        mine = rows_of(g)
        rows = mine.size
        gu = jnp.zeros((rows, 2 * hid), F32)
        dh = jnp.zeros((rows, hid), F32)
        for q in range(QUARTERS):
            cols = slice(q * qw, (q + 1) * qw)
            gu += jnp.dot(
                rb[0, q, part(g)].reshape(rows, qw), wcat[cols, :], preferred_element_type=F32
            )
            dh += jnp.dot(
                rb[1, q, part(g)].reshape(rows, qw), wdt[cols, :], preferred_element_type=F32
            )
        gate, upv = gu[:, 0:hid], gu[:, hid : 2 * hid]
        sig = jax.nn.sigmoid(gate)
        dgate = dh * upv * sig * (1.0 + gate * (1.0 - sig))
        dup = dh * gate * sig
        both = jnp.concatenate([dgate.astype(BF16), dup.astype(BF16)], axis=1)
        dd[mine, :] = both
        for q in range(QUARTERS):
            back = jnp.dot(
                both, wt[:, q * qw : (q + 1) * qw], preferred_element_type=F32
            )
            left = back[:, 0:wide]
            right = back[:, wide:qw]
            if narrow < wide:
                right = jnp.concatenate([right, jnp.zeros((rows, wide - narrow), F32)], axis=1)
            keep[q, mine] = jnp.where(is_x, left, right)
            sr1[q, mine] = jnp.where(is_x, right, left).astype(BF16)
        go(remote(sr1.at[:, mine], rr1.at[:, mine], s1_sem.at[g], r1_sem.at[g], dp=other))

    def stage_chip(g):
        mine = rows_of(g)
        landed(rr1.at[:, mine], r1_sem.at[g])
        for q in range(QUARTERS):
            sr2[q, mine] = (keep[q, mine] + rr1[q, mine].astype(F32)).astype(BF16)
        for j in range(1, QUARTERS):
            to = rem(y + j, QUARTERS)
            go(remote(
                sr2.at[to, mine], rr2.at[j - 1, mine], s2_sem.at[g, j - 1], r2_sem.at[g, j - 1],
                dp=to * CORES + core,
            ))

    def stage_back(g):
        mine = rows_of(g)
        for j in range(1, QUARTERS):
            landed(rr2.at[j - 1, mine], r2_sem.at[g, j - 1])
        total = keep[y, mine] + rr1[y, mine].astype(F32)
        for j in range(1, QUARTERS):
            total += rr2[j - 1, mine].astype(F32)
        total = total.astype(BF16)
        sr3[part(g)] = total.reshape(mine.size // most, most, wide)
        if starts[g] <= own_slot < starts[g + 1]:
            at = (own_slot - starts[g]) * most
            rr3[own_slot] = total[at : at + most]
        exchange(g, -1, sr3, rr3, s3_sem, r3_sem)

    def weight_grads(q):
        grads = lax.dot_general(
            rb[0, q].reshape(experts * most, qw), dd[...], TN, preferred_element_type=F32
        )
        out_g[0, q * qw : (q + 1) * qw, :] = grads[:, 0:hid].astype(BF16)
        out_u[0, q * qw : (q + 1) * qw, :] = grads[:, hid : 2 * hid].astype(BF16)

    def stages_of(g):
        tail = [stage_compute, stage_chip, stage_back]
        return [stage_own, stage_near] + ([stage_far] if g < RELAYED else []) + tail

    for stage, g in PLAN if parts == len(SIZES) else default_plan(parts):
        (stage_own, stage_near, stage_compute, stage_chip, stage_back, stage_far)[stage](g)
        if stage == 2 and g == parts - 1:
            weight_grads(0)
        if stage == 3 and g == parts - 1:
            weight_grads(1)
    weight_grads(2)
    weight_grads(3)

    for copy in sent_a + pending:
        copy.wait_send()
    for g in range(parts):
        arrived(g, sb, sb_sem.at[g])

    summed = jnp.zeros((toks, wide), F32)
    for g in range(parts):
        arrived(g, rr3, r3_sem.at[g])
        summed += jnp.dot(
            sel_ref[:, starts[g] * most : starts[g + 1] * most],
            rr3[part(g)].reshape(rows_of(g).size, wide),
            preferred_element_type=F32,
        )
    sf[...] = summed.astype(BF16).reshape(groups, per, wide)
    rf[d] = sf[d]
    for j in range(1, groups):
        p = rem(d + j, groups)
        go(remote(sf.at[p], rf.at[d], sf_sem.at[j - 1], rf_sem.at[j - 1], dp=p))
    for g in range(parts):
        arrived(g, sr3, s3_sem.at[g])
    for j in range(1, groups):
        landed(rf.at[rem(d + groups - j, groups)], rf_sem.at[j - 1])
    for p in range(groups):
        at, size = p // CORES * qw + p % CORES * wide, (wide, narrow)[p % CORES]
        out_t[0, :, at : at + size] = rf[p, :, 0:size]
    for copy in pending[-(groups - 1) :]:
        copy.wait_send()


def on_device(z_size, tokens, grad_out, routes, gate_scores, w_gate, w_up, w_down):
    groups = lax.axis_size("dp")
    experts = lax.axis_size("expert")
    per, width = tokens.shape[1:]
    hid = w_gate.shape[2]
    toks = per * groups
    c = shape_of(experts, z_size, width, toks, routes.shape[2], hid)
    most, qw, wide, parts = c["most"], c["qw"], c["wide"], len(c["starts"]) - 1
    rows = experts * most
    vmem = pl.BlockSpec(memory_space=pltpu.VMEM)
    hbm = pl.BlockSpec(memory_space=pl.ANY)
    dma = pltpu.SemaphoreType.DMA
    return pl.pallas_call(
        functools.partial(kernel, c),
        out_shape=(
            jax.ShapeDtypeStruct(tokens.shape, BF16),
            jax.ShapeDtypeStruct(w_gate.shape, BF16),
            jax.ShapeDtypeStruct(w_up.shape, BF16),
        ),
        in_specs=[hbm] * 7,
        out_specs=(vmem, vmem, vmem),
        scratch_shapes=[
            pltpu.VMEM((width, 2 * hid), BF16),
            pltpu.VMEM((hid, width), BF16),
            pltpu.VMEM((2 * hid, width), BF16),
            pltpu.VMEM((width, hid), BF16),
            pltpu.VMEM((groups, per, qw + 256), BF16),
            pltpu.VMEM((groups, per, qw + 256), BF16),
            pltpu.VMEM((experts, most, qw), BF16),
            pltpu.VMEM((CORES, QUARTERS, experts, most, qw), BF16),
            pltpu.VMEM((experts * most, 2 * hid), BF16),
            pltpu.VMEM((QUARTERS, rows, wide), F32),
            pltpu.VMEM((QUARTERS, rows, wide), BF16),
            pltpu.VMEM((QUARTERS, rows, wide), BF16),
            pltpu.VMEM((QUARTERS, rows, wide), BF16),
            pltpu.VMEM((QUARTERS - 1, rows, wide), BF16),
            pltpu.VMEM((experts, most, wide), BF16),
            pltpu.VMEM((experts, most, wide), BF16),
            pltpu.VMEM((groups, per, wide), BF16),
            pltpu.VMEM((groups, per, wide), BF16),
            pltpu.VMEM((toks, experts * most), BF16),
            pltpu.VMEM(tokens.shape, BF16),
            pltpu.VMEM(grad_out.shape, BF16),
            pltpu.VMEM(routes.shape, jnp.int32),
            pltpu.VMEM(gate_scores.shape, BF16),
            dma((4,)),
            dma((3,)),
            pltpu.SemaphoreType.REGULAR,
            dma((groups - 1,)),
            dma((groups - 1,)),
            dma((parts,)),
            dma((parts,)),
            dma((parts, 4)),
            dma((parts, 4)),
            dma((parts, 4)),
            dma((parts, 4)),
            dma((parts,)),
            dma((parts,)),
            dma((parts, 3)),
            dma((parts, 3)),
            dma((parts,)),
            dma((parts,)),
            dma((groups - 1,)),
            dma((groups - 1,)),
        ],
        compiler_params=pltpu.CompilerParams(
            collective_id=0, has_side_effects=True, vmem_limit_bytes=60 * 1024 * 1024
        ),
        cost_estimate=pl.CostEstimate(
            flops=14 * experts * most * width * hid, bytes_accessed=10 * width * hid,
            transcendentals=experts * most * hid,
        ),
    )(tokens, grad_out, routes, gate_scores, w_gate, w_up, w_down)


def solution(mesh):
    placed = (
        P("expert", "dp", None),
        P("expert", "dp", None),
        P("expert", "dp", None),
        P("expert", "dp", None),
        P("expert", None, "dp"),
        P("expert", None, "dp"),
        P("expert", "dp", None),
    )
    z_size = 16 if mesh.shape["expert"] == 64 else 2
    return jax.shard_map(
        functools.partial(on_device, z_size),
        mesh=mesh,
        in_specs=placed,
        out_specs=(P("expert", "dp", None), P("expert", None, "dp"), P("expert", None, "dp")),
        check_vma=False,
    )
```

```python
import functools

import jax
import jax.numpy as jnp
from jax import lax
from jax.experimental import pallas as pl
from jax.experimental.pallas import tpu as pltpu
from jax.sharding import PartitionSpec as P

ROUTED = 256
CORES = 2
QUARTERS = 4
SIZES = (3, 3, 3, 3, 2, 2)
RELAYED = 0
PLAN = (
    (0, 0), (0, 1), (1, 0), (0, 2), (2, 0), (1, 1), (3, 0), (2, 1),
    (0, 3), (1, 2), (3, 1), (2, 2), (4, 0), (0, 4), (3, 2), (1, 3),
    (2, 3), (4, 1), (0, 5), (3, 3), (1, 4), (2, 4), (4, 2), (3, 4),
    (1, 5), (2, 5), (4, 3), (3, 5), (4, 4), (4, 5),
)
MESH = pl.DeviceIdType.MESH
F32, BF16 = jnp.float32, jnp.bfloat16
NT = (((1,), (1,)), ((), ()))
TN = (((0,), (0,)), ((), ()))


def order_of(z_size):
    steps = [0]
    for h in range(1, z_size // 2 + 1):
        steps += [h] if 2 * h == z_size else [h, -h]
    far = sorted(steps, key=lambda s: (-abs(s), -s))
    return far[::-1]


def default_plan(parts):
    stages = (0, 1, 5, 2, 3, 4) if RELAYED else (0, 1, 2, 3, 4)
    return [(stage, g) for g in range(parts) for stage in stages]


def shape_of(mesh_experts, columns_z, width, tok_col, top, hidden):
    z_size = columns_z
    x_size = mesh_experts // z_size
    most = max(2, 2 * tok_col * top // ROUTED)
    quarter = width // QUARTERS
    tiles = quarter // 128
    wide = (tiles + 1) // 2 * 128
    sizes = SIZES if sum(SIZES) == z_size else (1,) * z_size
    starts = [sum(sizes[:g]) * x_size for g in range(len(sizes) + 1)]
    return dict(
        order=order_of(z_size), xs=x_size, zs=z_size, most=most, qw=quarter, wide=wide, starts=starts,
        experts=mesh_experts, toks=tok_col, top=top, hid=hidden,
    )


def kernel(
    c, tok_hbm, dy_hbm, routes_hbm, scores_hbm, wg_hbm, wu_hbm, wd_hbm,
    out_t, out_g, out_u,
    wcat, wd, wt, wdt, sa, ra, sb, rb, dd, keep, sr1, rr1, sr2, rr2, sr3, rr3, sf, rf, sel_ref,
    tok_ref, dy_ref, routes_ref, scores_ref, in_sem, w_sem, ring_sem, sa_sem, ra_sem, sb_sem, rb_sem,
    sy_sem, ry_sem, sc_sem, rc_sem, s1_sem, r1_sem, s2_sem, r2_sem, s3_sem, r3_sem,
    sf_sem, rf_sem,
):
    xs, zs, most, qw, wide, starts = c["xs"], c["zs"], c["most"], c["qw"], c["wide"], c["starts"]
    experts, toks, hid = c["experts"], c["toks"], c["hid"]
    parts = len(starts) - 1
    narrow = qw - wide
    order = c["order"]
    own_slot = order.index(0) * xs
    top = c["top"]
    groups = CORES * QUARTERS
    per = toks // groups
    d = lax.axis_index("dp")
    e = lax.axis_index("expert")
    rem, div = lax.rem, lax.div
    y, core = div(d, CORES), rem(d, CORES)
    x, z = div(e, zs), rem(e, zs)
    other = y * CORES + (1 - core)
    up_y, down_y = rem(y + 1, QUARTERS), rem(y + QUARTERS - 1, QUARTERS)
    far_y = rem(y + 2, QUARTERS)
    up, down = up_y * CORES + core, down_y * CORES + core

    def remote(src, dst, send, recv, **where):
        return pltpu.make_async_remote_copy(
            src_ref=src, dst_ref=dst, send_sem=send, recv_sem=recv,
            device_id=where, device_id_type=MESH,
        )

    def landed(ref, sem):
        pltpu.make_async_copy(ref, ref, sem).wait()

    small = [
        pltpu.make_async_copy(src, dst, in_sem.at[i])
        for i, (src, dst) in enumerate((
            (routes_hbm, routes_ref), (scores_hbm, scores_ref),
            (tok_hbm, tok_ref), (dy_hbm, dy_ref),
        ))
    ]
    for load in small:
        load.start()
    loads = [
        pltpu.make_async_copy(wg_hbm.at[0], wcat.at[:, 0:hid], w_sem.at[0]),
        pltpu.make_async_copy(wu_hbm.at[0], wcat.at[:, hid : 2 * hid], w_sem.at[1]),
        pltpu.make_async_copy(wd_hbm.at[0], wd, w_sem.at[2]),
    ]
    for load in loads:
        load.start()

    if narrow < wide:
        rr2[:, :, narrow:wide] = jnp.zeros(rr2.shape[:2] + (wide - narrow,), BF16)

    barrier = pltpu.get_barrier_semaphore()

    def greet(j, carry):
        dz = zs // 2 + div(j + 1, 2) * (2 * rem(j, 2) - 1)
        pl.semaphore_signal(
            barrier, inc=1, device_id={"expert": x * zs + rem(z + dz, zs)}, device_id_type=MESH
        )
        return carry

    lax.fori_loop(0, zs - 1, greet, 0)
    for j in range(1, groups):
        pl.semaphore_signal(
            barrier, inc=1, device_id={"dp": rem(d + j, groups)}, device_id_type=MESH
        )

    for j in range(1, xs):
        pl.semaphore_signal(
            barrier, inc=1, device_id={"expert": rem(x + j, xs) * zs + z}, device_id_type=MESH
        )


    for load in small:
        load.wait()
    for p in range(groups):
        source = tok_ref if p % CORES == 0 else dy_ref
        at = p // CORES * qw
        sa[p, :, 0:qw] = source[0, :, at : at + qw]
        sa[p, :, qw : qw + top] = routes_ref[0].astype(F32).astype(BF16)
        sa[p, :, qw + 128 : qw + 128 + top] = scores_ref[0]
    ra[d] = sa[d]
    pl.semaphore_wait(barrier, groups - 1 + xs - 1 + zs - 1)

    sent_a = []
    for j in range(1, groups):
        p = rem(d + j, groups)
        sent_a.append(remote(sa.at[p], ra.at[d], sa_sem.at[j - 1], ra_sem.at[j - 1], dp=p))
        sent_a[-1].start()
    for j in range(1, xs):
        pl.semaphore_signal(
            ring_sem, inc=1, device_id={"expert": rem(x + j, xs) * zs + z}, device_id_type=MESH
        )

    shape = (toks, experts * most)
    row = lax.broadcasted_iota(jnp.int32, shape, 1)
    place_of = row & (most - 1)
    slot_of = row >> (most.bit_length() - 1)
    dx_of = slot_of & (xs - 1)
    k_of = slot_of >> (xs.bit_length() - 1)
    dz_of = jnp.zeros(shape, jnp.int32)
    for k, dz in enumerate(order):
        dz_of = jnp.where(k_of == k, dz, dz_of)
    target = (((x + dx_of) & (xs - 1)) * zs + ((z + dz_of) & (zs - 1))).astype(F32)
    before = (
        lax.broadcasted_iota(jnp.int32, (toks, toks), 1)
        < lax.broadcasted_iota(jnp.int32, (toks, toks), 0)
    ).astype(F32).astype(BF16)
    for j in range(1, groups):
        landed(ra.at[rem(d + groups - j, groups)], ra_sem.at[j - 1])
    route = ra[:, :, qw : qw + 128].reshape(toks, 128).astype(F32)
    score = ra[:, :, qw + 128 : qw + 256].reshape(toks, 128).astype(F32)
    hit = jnp.zeros(shape, F32)
    weight = jnp.zeros(shape, F32)
    for k in range(c["top"]):
        same = route[:, k : k + 1] == target
        hit = jnp.where(same, 1.0, hit)
        weight = jnp.where(same, score[:, k : k + 1], weight)
    place = jnp.dot(before, hit.astype(BF16), preferred_element_type=F32)
    chosen = jnp.where(place == place_of.astype(F32), hit, 0.0)
    sel_ref[...] = chosen.astype(BF16)
    is_x = core == 0
    scaled = jnp.where(is_x, chosen, chosen * weight).astype(BF16)

    picked = lax.dot_general(
        scaled, ra[:, :, 0:qw].reshape(toks, qw), TN, preferred_element_type=F32
    ).astype(BF16)
    sb[...] = picked.reshape(experts, most, qw)
    rb[core, y, own_slot] = picked[own_slot * most : (own_slot + 1) * most]

    pl.semaphore_wait(ring_sem, xs - 1)
    def by_width(act):
        pl.when(is_x)(lambda: act(wide))
        pl.when(jnp.logical_not(is_x))(lambda: act(narrow))

    def exchange(g, sign, src, dst, send, recv):
        for k in range(starts[g] // xs, starts[g + 1] // xs):
            to_z = rem(z + sign * order[k] + zs, zs)

            def send_rows(dx, carry, k=k, to_z=to_z):
                to = rem(x + sign * dx + xs, xs) * zs + to_z
                remote(
                    src.at[k * xs + dx], dst.at[k * xs + dx], send.at[g], recv.at[g], expert=to
                ).start()
                return carry

            lax.fori_loop(1 if order[k] == 0 else 0, xs, send_rows, 0)

    mine_rb = rb.at[core, y]
    for g in range(parts):
        exchange(g, 1, sb, mine_rb, sb_sem, rb_sem)

    def arrived(g, ref, sem):
        low, high = starts[g], starts[g + 1]
        if low <= own_slot < high:
            if own_slot > low:
                landed(ref.at[pl.ds(low, own_slot - low)], sem)
            low = own_slot + 1
        landed(ref.at[pl.ds(low, high - low)], sem)

    def part(g, piece=None):
        low, high = starts[g], starts[g + 1]
        middle = (low + high) // 2
        if piece is not None:
            low, high = (low, middle) if piece == 0 else (middle, high)
        return pl.ds(low, high - low)

    def rows_of(g):
        return pl.ds(starts[g] * most, (starts[g + 1] - starts[g]) * most)

    for load in loads:
        load.wait()
    for q in range(QUARTERS):
        cols = slice(q * qw, (q + 1) * qw)
        wt[:, cols] = wcat[cols, :].T
        wdt[cols, :] = wd[:, cols].T
    pending = []

    def go(copy):
        copy.start()
        pending.append(copy)

    def stage_own(g):
        arrived(g, mine_rb, rb_sem.at[g])
        mine = rb.at[core, y, part(g)]
        go(remote(mine, mine, sy_sem.at[g, 0], ry_sem.at[g, 0], dp=up))
        go(remote(mine, mine, sy_sem.at[g, 1], ry_sem.at[g, 1], dp=down))
        if g >= RELAYED:
            go(remote(mine, mine, sy_sem.at[g, 2], ry_sem.at[g, 2], dp=far_y * CORES + core))
        go(remote(mine, mine, sc_sem.at[g, 0], rc_sem.at[g, 0], dp=other))

    def stage_near(g):
        low = rb.at[core, down_y, part(g)]
        landed(low, ry_sem.at[g, 0])
        if g < RELAYED:
            piece = rb.at[core, down_y, part(g, 0)]
            go(remote(piece, piece, sy_sem.at[g, 2], ry_sem.at[g, 2], dp=up))
        go(remote(low, low, sc_sem.at[g, 1], rc_sem.at[g, 1], dp=other))
        high = rb.at[core, up_y, part(g)]
        landed(high, ry_sem.at[g, 1])
        if g < RELAYED:
            piece = rb.at[core, up_y, part(g, 1)]
            go(remote(piece, piece, sy_sem.at[g, 3], ry_sem.at[g, 3], dp=down))
        go(remote(high, high, sc_sem.at[g, 2], rc_sem.at[g, 2], dp=other))
        if g >= RELAYED:
            stage_far(g)

    def stage_far(g):
        whole = rb.at[core, far_y, part(g)]
        if g < RELAYED:
            landed(rb.at[core, far_y, part(g, 0)], ry_sem.at[g, 2])
            landed(rb.at[core, far_y, part(g, 1)], ry_sem.at[g, 3])
        else:
            landed(whole, ry_sem.at[g, 2])
        go(remote(whole, whole, sc_sem.at[g, 3], rc_sem.at[g, 3], dp=other))

    def stage_compute(g):
        for at, which in enumerate((y, down_y, up_y, far_y)):
            landed(rb.at[1 - core, which, part(g)], rc_sem.at[g, at])
        mine = rows_of(g)
        rows = mine.size
        gu = jnp.zeros((rows, 2 * hid), F32)
        dh = jnp.zeros((rows, hid), F32)
        for q in range(QUARTERS):
            cols = slice(q * qw, (q + 1) * qw)
            gu += jnp.dot(
                rb[0, q, part(g)].reshape(rows, qw), wcat[cols, :], preferred_element_type=F32
            )
            dh += jnp.dot(
                rb[1, q, part(g)].reshape(rows, qw), wdt[cols, :], preferred_element_type=F32
            )
        gate, upv = gu[:, 0:hid], gu[:, hid : 2 * hid]
        sig = jax.nn.sigmoid(gate)
        dgate = dh * upv * sig * (1.0 + gate * (1.0 - sig))
        dup = dh * gate * sig
        both = jnp.concatenate([dgate.astype(BF16), dup.astype(BF16)], axis=1)
        dd[mine, :] = both
        for q in range(QUARTERS):
            back = jnp.dot(
                both, wt[:, q * qw : (q + 1) * qw], preferred_element_type=F32
            )
            left = back[:, 0:wide]
            right = back[:, wide:qw]
            if narrow < wide:
                right = jnp.concatenate([right, jnp.zeros((rows, wide - narrow), F32)], axis=1)
            keep[q, mine] = jnp.where(is_x, left, right)
            sr1[q, mine] = jnp.where(is_x, right, left).astype(BF16)
        go(remote(sr1.at[:, mine], rr1.at[:, mine], s1_sem.at[g], r1_sem.at[g], dp=other))

    def stage_chip(g):
        mine = rows_of(g)
        landed(rr1.at[:, mine], r1_sem.at[g])
        for q in range(QUARTERS):
            sr2[q, mine] = (keep[q, mine] + rr1[q, mine].astype(F32)).astype(BF16)
        def send_chip(cols):
            for j in range(1, QUARTERS):
                to = rem(y + j, QUARTERS)
                remote(
                    sr2.at[to, mine, 0:cols], rr2.at[j - 1, mine, 0:cols],
                    s2_sem.at[g, j - 1], r2_sem.at[g, j - 1], dp=to * CORES + core,
                ).start()

        by_width(send_chip)

    def landed_chip(g, ref, sems):
        def wait(cols):
            for j in range(1, QUARTERS):
                landed(ref.at[j - 1, rows_of(g), 0:cols], sems.at[g, j - 1])

        by_width(wait)

    def stage_back(g):
        mine = rows_of(g)
        landed_chip(g, rr2, r2_sem)
        total = keep[y, mine] + rr1[y, mine].astype(F32)
        for j in range(1, QUARTERS):
            total += rr2[j - 1, mine].astype(F32)
        total = total.astype(BF16)
        sr3[part(g)] = total.reshape(mine.size // most, most, wide)
        if starts[g] <= own_slot < starts[g + 1]:
            at = (own_slot - starts[g]) * most
            rr3[own_slot] = total[at : at + most]
        exchange(g, -1, sr3, rr3, s3_sem, r3_sem)

    def weight_grads(q):
        grads = lax.dot_general(
            rb[0, q].reshape(experts * most, qw), dd[...], TN, preferred_element_type=F32
        )
        out_g[0, q * qw : (q + 1) * qw, :] = grads[:, 0:hid].astype(BF16)
        out_u[0, q * qw : (q + 1) * qw, :] = grads[:, hid : 2 * hid].astype(BF16)

    def stages_of(g):
        tail = [stage_compute, stage_chip, stage_back]
        return [stage_own, stage_near] + ([stage_far] if g < RELAYED else []) + tail

    for stage, g in PLAN if parts == len(SIZES) else default_plan(parts):
        (stage_own, stage_near, stage_compute, stage_chip, stage_back, stage_far)[stage](g)
        if stage == 2 and g == parts - 1:
            weight_grads(0)
        if stage == 3 and g == parts - 1:
            weight_grads(1)
    weight_grads(2)
    weight_grads(3)

    for copy in sent_a + pending:
        copy.wait_send()
    for g in range(parts):
        arrived(g, sb, sb_sem.at[g])
        landed_chip(g, sr2, s2_sem)

    summed = jnp.zeros((toks, wide), F32)
    for g in range(parts):
        arrived(g, rr3, r3_sem.at[g])
        summed += jnp.dot(
            sel_ref[:, starts[g] * most : starts[g + 1] * most],
            rr3[part(g)].reshape(rows_of(g).size, wide),
            preferred_element_type=F32,
        )
    sf[...] = summed.astype(BF16).reshape(groups, per, wide)
    rf[d] = sf[d]
    for j in range(1, groups):
        p = rem(d + j, groups)
        go(remote(sf.at[p], rf.at[d], sf_sem.at[j - 1], rf_sem.at[j - 1], dp=p))
    for g in range(parts):
        arrived(g, sr3, s3_sem.at[g])
    for j in range(1, groups):
        landed(rf.at[rem(d + groups - j, groups)], rf_sem.at[j - 1])
    for p in range(groups):
        at, size = p // CORES * qw + p % CORES * wide, (wide, narrow)[p % CORES]
        out_t[0, :, at : at + size] = rf[p, :, 0:size]
    for copy in pending[-(groups - 1) :]:
        copy.wait_send()


def on_device(z_size, tokens, grad_out, routes, gate_scores, w_gate, w_up, w_down):
    groups = lax.axis_size("dp")
    experts = lax.axis_size("expert")
    per, width = tokens.shape[1:]
    hid = w_gate.shape[2]
    toks = per * groups
    c = shape_of(experts, z_size, width, toks, routes.shape[2], hid)
    most, qw, wide, parts = c["most"], c["qw"], c["wide"], len(c["starts"]) - 1
    rows = experts * most
    vmem = pl.BlockSpec(memory_space=pltpu.VMEM)
    hbm = pl.BlockSpec(memory_space=pl.ANY)
    dma = pltpu.SemaphoreType.DMA
    return pl.pallas_call(
        functools.partial(kernel, c),
        out_shape=(
            jax.ShapeDtypeStruct(tokens.shape, BF16),
            jax.ShapeDtypeStruct(w_gate.shape, BF16),
            jax.ShapeDtypeStruct(w_up.shape, BF16),
        ),
        in_specs=[hbm] * 7,
        out_specs=(vmem, vmem, vmem),
        scratch_shapes=[
            pltpu.VMEM((width, 2 * hid), BF16),
            pltpu.VMEM((hid, width), BF16),
            pltpu.VMEM((2 * hid, width), BF16),
            pltpu.VMEM((width, hid), BF16),
            pltpu.VMEM((groups, per, qw + 256), BF16),
            pltpu.VMEM((groups, per, qw + 256), BF16),
            pltpu.VMEM((experts, most, qw), BF16),
            pltpu.VMEM((CORES, QUARTERS, experts, most, qw), BF16),
            pltpu.VMEM((experts * most, 2 * hid), BF16),
            pltpu.VMEM((QUARTERS, rows, wide), F32),
            pltpu.VMEM((QUARTERS, rows, wide), BF16),
            pltpu.VMEM((QUARTERS, rows, wide), BF16),
            pltpu.VMEM((QUARTERS, rows, wide), BF16),
            pltpu.VMEM((QUARTERS - 1, rows, wide), BF16),
            pltpu.VMEM((experts, most, wide), BF16),
            pltpu.VMEM((experts, most, wide), BF16),
            pltpu.VMEM((groups, per, wide), BF16),
            pltpu.VMEM((groups, per, wide), BF16),
            pltpu.VMEM((toks, experts * most), BF16),
            pltpu.VMEM(tokens.shape, BF16),
            pltpu.VMEM(grad_out.shape, BF16),
            pltpu.VMEM(routes.shape, jnp.int32),
            pltpu.VMEM(gate_scores.shape, BF16),
            dma((4,)),
            dma((3,)),
            pltpu.SemaphoreType.REGULAR,
            dma((groups - 1,)),
            dma((groups - 1,)),
            dma((parts,)),
            dma((parts,)),
            dma((parts, 4)),
            dma((parts, 4)),
            dma((parts, 4)),
            dma((parts, 4)),
            dma((parts,)),
            dma((parts,)),
            dma((parts, 3)),
            dma((parts, 3)),
            dma((parts,)),
            dma((parts,)),
            dma((groups - 1,)),
            dma((groups - 1,)),
        ],
        compiler_params=pltpu.CompilerParams(
            collective_id=0, has_side_effects=True, vmem_limit_bytes=60 * 1024 * 1024
        ),
        cost_estimate=pl.CostEstimate(
            flops=14 * experts * most * width * hid, bytes_accessed=10 * width * hid,
            transcendentals=experts * most * hid,
        ),
    )(tokens, grad_out, routes, gate_scores, w_gate, w_up, w_down)


def solution(mesh):
    placed = (
        P("expert", "dp", None),
        P("expert", "dp", None),
        P("expert", "dp", None),
        P("expert", "dp", None),
        P("expert", None, "dp"),
        P("expert", None, "dp"),
        P("expert", "dp", None),
    )
    z_size = 16 if mesh.shape["expert"] == 64 else 2
    return jax.shard_map(
        functools.partial(on_device, z_size),
        mesh=mesh,
        in_specs=placed,
        out_specs=(P("expert", "dp", None), P("expert", None, "dp"), P("expert", None, "dp")),
        check_vma=False,
    )
```
